32 devices in a mesh: region: 2 (over y), slab: 16 (over z, x, core).
Axes of the slice: x: 2, y: 2, z: 4, core: 2. Of those that a mesh axis runs over, the one named last changes fastest.
Arguments:
- magnetic: float32 [3, 256, 64, 256], P(None, 'slab', None, 'region'), may hold values from -6 to 6
- velocity: float32 [3, 256, 64, 256], P(None, 'slab', None, 'region'), may hold values from -12 to 12
- wall_response: float32 [256, 256, 256], P(('region', 'slab')), may hold values from -0.375 to 0.375
- mode_slots: int32 [256], replicated, may hold values from 0 to 255, each once
- wall_layers: int32 [256], P('region'), may hold values from 1 to 8
Outputs:
- magnetic_next: float32 [3, 256, 64, 256], P(None, 'slab', None, 'region')
- wall_flux: float32 [2, 256, 256], P(None, 'slab', 'region')
The draws below stay inside these ranges and needn't reach their ends.
Inputs may be any that keep to these rules, and one draw needn't show every extreme that they name: `mode_slots`: each slot names a different mode.
All inputs are finite; a program needn't handle non-finite values.
Results may differ from the reference program's by a relative error of at most 0.00007.
Values sent between devices are 32-bit elements; how exact they have to be, the bound alone decides.
A program may use at most 128 MiB of HBM per device.

```python
import math
import jax
import jax.numpy as jnp
from jax import lax

NR = 64
LW = 8
NZ = 256
NPHI = 256


def set_ends(array, rng, low, top_value):
    shape = array.shape
    index_at = [jax.random.randint(jax.random.fold_in(rng, axis), (), 0, shape[axis]) for axis in range(len(shape))]
    array = array.at[tuple(index_at)].set(low)
    longest = shape.index(max(shape))
    index_at[longest] = (index_at[longest] + 1) % shape[longest]
    return array.at[tuple(index_at)].set(top_value)


def levels(key, dims, pieces, least, top_value):
    factor_of, own = 1.0, jax.random.fold_in(key, 6)
    for position, parts in pieces:
        heights = jnp.exp(jax.random.uniform(jax.random.fold_in(own, position), (parts,), jnp.float32, least / len(pieces), top_value / len(pieces)))
        factor_of = factor_of * jnp.repeat(heights, dims[position] // parts).reshape([-1 if axis == position else 1 for axis in range(len(dims))])
    return factor_of


def scatter_about(key, extent, width, limit, shards=(), held_as=jnp.bfloat16):
    values = jax.random.normal(key, extent, jnp.float32) * width
    if len(shards) > 0:
        values = levels(key, extent, shards, -0.22, 0.18) * values
    return jnp.clip(values, min=-limit, max=limit).astype(held_as)


def setup_inputs(seed: int = 0) -> dict:
    splits = jax.random.split(jax.random.key(seed), 6)
    magnetic = scatter_about(splits[0], (3, NZ, NR, NPHI), 1.0, 6.0, ((1, 16), (3, 2)), jnp.float32)
    velocity = scatter_about(splits[1], (3, NZ, NR, NPHI), 2.0, 12.0, ((1, 16), (3, 2)), jnp.float32)
    wall_response = scatter_about(splits[2], (NPHI, NZ, NZ), NZ ** -0.5, 0.375, ((0, 32),), jnp.float32)
    mode_slots = jax.random.permutation(splits[3], NPHI).astype(jnp.int32)
    wall_layers = set_ends(jax.random.randint(splits[4], (NPHI,), 1, LW + 1), jax.random.fold_in(splits[4], 1), 1, LW).astype(jnp.int32)
    return {"magnetic": magnetic, "velocity": velocity, "wall_response": wall_response, "mode_slots": mode_slots, "wall_layers": wall_layers}


TIME_STEP = 3.0e-4
DIFFUSIVITY = 1.0e-3
RADIAL_STEP = 1.0 / 384.0
AXIAL_STEP = 1.0 / 768.0
HIGHEST = lax.Precision.HIGHEST


def basis_table(modes, cells, azimuth_total):
    frequency = (modes + 1) // 2
    phase = (frequency[:, None] * (2 * cells[None, :] + 1)) % (2 * azimuth_total)
    angle = phase.astype(jnp.float32) * (math.pi / azimuth_total)
    return jnp.where((modes % 2 == 1)[:, None], jnp.sin(angle), jnp.cos(angle))


def mode_weight(modes, azimuth_total):
    single = (modes == 0) | (modes == azimuth_total - 1)
    return jnp.where(single, 1.0, 2.0).astype(jnp.float32) / azimuth_total


def radius_column(radial_cells):
    index = jnp.arange(radial_cells).astype(jnp.float32)
    return (1.0 - (radial_cells - index - 0.5) * RADIAL_STEP)[:, None]


def advance(center_b, center_u, radial_b, radial_u, azimuth_b, azimuth_u, axial_b, axial_u, radius, angle_step):
    inv_radial = 1.0 / (2.0 * RADIAL_STEP)
    inv_azimuth = 1.0 / (2.0 * radius * angle_step)
    inv_axial = 1.0 / (2.0 * AXIAL_STEP)
    grad_b = ((radial_b[0] - radial_b[1]) * inv_radial, (azimuth_b[0] - azimuth_b[1]) * inv_azimuth, (axial_b[0] - axial_b[1]) * inv_axial)
    grad_u = ((radial_u[0] - radial_u[1]) * inv_radial, (azimuth_u[0] - azimuth_u[1]) * inv_azimuth, (axial_u[0] - axial_u[1]) * inv_axial)
    laplace = (radial_b[0] - 2.0 * center_b + radial_b[1]) / RADIAL_STEP ** 2
    laplace = laplace + grad_b[0] / radius
    laplace = laplace + (azimuth_b[0] - 2.0 * center_b + azimuth_b[1]) / (radius * angle_step) ** 2
    laplace = laplace + (axial_b[0] - 2.0 * center_b + axial_b[1]) / AXIAL_STEP ** 2
    carried = center_u[0] * grad_b[0] + center_u[1] * grad_b[1] + center_u[2] * grad_b[2]
    stretched = center_b[0] * grad_u[0] + center_b[1] * grad_u[1] + center_b[2] * grad_u[2]
    return center_b + TIME_STEP * (DIFFUSIVITY * laplace - carried + stretched)


def pad_around(values):
    padded = jnp.pad(values, ((0, 0), (1, 1), (0, 0), (0, 0)))
    return jnp.concatenate([padded[..., -1:], padded, padded[..., :1]], -1)


def neighbours(padded):
    center = padded[:, 1:-1, 1:-1, 1:-1]
    radial = (padded[:, 1:-1, 2:, 1:-1], padded[:, 1:-1, :-2, 1:-1])
    azimuth = (padded[:, 1:-1, 1:-1, 2:], padded[:, 1:-1, 1:-1, :-2])
    axial = (padded[:, 2:, 1:-1, 1:-1], padded[:, :-2, 1:-1, 1:-1])
    return center, radial, azimuth, axial


def reference(magnetic, velocity, wall_response, mode_slots, wall_layers):
    radial_cells = magnetic.shape[2]
    azimuth_total = magnetic.shape[3]
    trace = magnetic[1:3, :, radial_cells - 1, :]
    cells = jnp.arange(azimuth_total, dtype=jnp.int32)
    table = basis_table(mode_slots, cells, azimuth_total)
    coefficients = jnp.einsum("sk,czk->scz", table, trace, precision=HIGHEST)
    responses = jnp.einsum("szy,scy->scz", wall_response, coefficients, precision=HIGHEST)
    weighted = table * mode_weight(mode_slots, azimuth_total)[:, None]
    wall_flux = jnp.einsum("sk,scz->czk", weighted, responses, precision=HIGHEST)
    thickness = wall_layers.astype(jnp.float32) / LW
    ghost = jnp.concatenate([magnetic[0:1, :, radial_cells - 1, :], trace - thickness * wall_flux], 0)
    magnetic_ext = jnp.concatenate([magnetic[:, :, :1], magnetic, ghost[:, :, None]], 2)
    velocity_ext = jnp.concatenate([velocity[:, :, :1], velocity, velocity[:, :, -1:]], 2)
    center_b, radial_b, azimuth_b, axial_b = neighbours(pad_around(magnetic_ext))
    center_u, radial_u, azimuth_u, axial_u = neighbours(pad_around(velocity_ext))
    radius = radius_column(radial_cells)
    angle_step = 2.0 * math.pi / azimuth_total
    magnetic_next = advance(center_b, center_u, radial_b, radial_u, azimuth_b, azimuth_u, axial_b, axial_u, radius, angle_step)
    return magnetic_next, wall_flux
```

```python
import functools
import math

import jax
import jax.numpy as jnp
from jax import lax
from jax.experimental import pallas as pl
from jax.experimental.pallas import tpu as pltpu
from jax.sharding import PartitionSpec as P

LW = 8
TIME_STEP = 0.0003
DIFFUSIVITY = 0.001
RADIAL_STEP = 1.0 / 384.0
AXIAL_STEP = 1.0 / 768.0
HIGHEST = lax.Precision.HIGHEST
MESH = pl.DeviceIdType.MESH
F32 = jnp.float32
BF16 = jnp.bfloat16

PAD = 8
LANES = 128


def iota(shape, dim):
    return lax.broadcasted_iota(jnp.int32, shape, dim)


def split(x):
    hi = x.astype(BF16)
    return hi, (x - hi.astype(F32)).astype(BF16)


def sine(t):
    s = t * t
    value = 1.0 / math.factorial(13)
    for n in (11, 9, 7, 5, 3, 1):
        sign = 1.0 if (n // 2) % 2 == 0 else -1.0
        value = value * s + sign / math.factorial(n)
    return value * t


def exact_dot(a, b, contract):
    return lax.dot_general(
        a, b, ((contract[0], contract[1]), ((), ())), precision=HIGHEST, preferred_element_type=F32
    )


def step_kernel(
    regions,
    slabs,
    mode_ref,
    layer_ref,
    mag_hbm,
    vel_hbm,
    wall_hbm,
    next_hbm,
    flux_ref,
    b_s,
    u_s,
    out_s,
    wall_s,
    whi_s,
    wlo_s,
    table_s,
    weighted_s,
    trace_s,
    blocks_s,
    radial_s,
    row_s,
    spread_s,
    send1,
    recv1,
    send2,
    recv2,
    pack_s,
    around_s,
    halo_s,
    load_sem,
    store_sem,
    a2a_send,
    a2a_recv,
    ax_send,
    ax_recv,
    az_send,
    az_recv,
):
    count = regions * slabs
    radial = mag_hbm.shape[2]
    axial = mag_hbm.shape[1]
    azimuth_total = mode_ref.shape[1]
    mode_count, nz, _ = wall_hbm.shape
    rows_each = send1.shape[1]
    slot_rows = count * rows_each
    per_row = LANES // (2 * axial)
    region = lax.axis_index("region")
    slab = lax.axis_index("slab")
    me = region * slabs + slab
    cells = pl.ds(PAD, radial)

    load_b = pltpu.make_async_copy(mag_hbm, b_s.at[:, 1 : axial + 1, cells, :], load_sem.at[0])
    load_u = pltpu.make_async_copy(vel_hbm, u_s.at[:, 1 : axial + 1, cells, :], load_sem.at[1])
    load_w = pltpu.make_async_copy(wall_hbm, wall_s, load_sem.at[2])
    load_b.start()
    load_u.start()
    load_w.start()

    barrier = pltpu.get_barrier_semaphore()

    @pl.loop(1, count)
    def _(i):
        other = lax.rem(me + i, count)
        pl.semaphore_signal(
            barrier,
            inc=1,
            device_id=(other // slabs, lax.rem(other, slabs)),
            device_id_type=MESH,
        )

    modes = mode_ref[...].astype(F32)
    padded = table_s.shape[0]
    shape = (padded, azimuth_total)
    chosen = jnp.where(iota(shape, 1) // per_row == iota(shape, 0), modes, 0.0)
    shape = (azimuth_total, per_row * LANES)
    picks = jnp.where(lax.rem(iota(shape, 0), per_row) == iota(shape, 1) // LANES, 1.0, 0.0)
    mode = exact_dot(chosen, picks, ((1,), (0,)))
    half = jnp.floor(mode * 0.5)
    odd = mode - 2.0 * half
    cell = region * LANES + lax.rem(iota(mode.shape, 1), LANES)
    turn = (half + odd) * (2 * cell + 1).astype(F32) - odd * (azimuth_total // 2)
    turn = turn * (0.5 / azimuth_total)
    turn = turn - jnp.floor(turn + 0.5)
    table = sine((0.25 - jnp.abs(turn)) * (2.0 * math.pi))
    table_s[...] = table
    single = (mode == 0.0) | (mode == azimuth_total - 1.0)
    weighted_s[...] = table * (jnp.where(single, 1.0, 2.0) / azimuth_total)

    shape = (radial, LANES)
    radius = 1.0 - (radial - iota(shape, 0).astype(F32) - 0.5) * RADIAL_STEP
    inverse = 1.0 / radius
    angle_step = 2.0 * math.pi / azimuth_total
    kr = TIME_STEP * DIFFUSIVITY / RADIAL_STEP**2
    kz = TIME_STEP * DIFFUSIVITY / AXIAL_STEP**2
    ar = TIME_STEP / (2.0 * RADIAL_STEP)
    az = TIME_STEP / (2.0 * AXIAL_STEP)
    kp = inverse * inverse * (TIME_STEP * DIFFUSIVITY / angle_step**2)
    radial_s[0] = inverse * (TIME_STEP / (2.0 * angle_step))
    radial_s[1] = kp
    radial_s[2] = inverse * (TIME_STEP * DIFFUSIVITY / (2.0 * RADIAL_STEP))
    radial_s[3] = (1.0 - 2.0 * kr - 2.0 * kz) - 2.0 * kp

    if slot_rows < padded:
        row_s[...] = jnp.zeros(row_s.shape, F32)
    blocks_s[...] = jnp.zeros(blocks_s.shape, F32)

    load_b.wait()
    for c in range(2):
        for z in range(axial):
            at = c * axial + z
            trace_s[at : at + 1, :] = b_s[c + 1, z + 1, PAD + radial - 1 : PAD + radial, :]
    trace = trace_s[...]
    for q in range(per_row):
        blocks_s[2 * axial * q : 2 * axial * (q + 1), LANES * q : LANES * (q + 1)] = trace
    coefficients = exact_dot(table_s[0:slot_rows, :], blocks_s[...], ((1,), (1,)))
    for o in range(count):
        send1[o] = coefficients[rows_each * o : rows_each * (o + 1)]
    recv1[pl.ds(me, 1)] = send1[pl.ds(me, 1)]

    pl.semaphore_wait(barrier, count - 1)

    @pl.loop(1, count)
    def _(i):
        other = lax.rem(me + i, count)
        pltpu.make_async_remote_copy(
            src_ref=send1.at[other],
            dst_ref=recv1.at[me],
            send_sem=a2a_send.at[0],
            recv_sem=a2a_recv.at[0],
            device_id=(other // slabs, lax.rem(other, slabs)),
            device_id_type=MESH,
        ).start()

    load_u.wait()

    def axial_copy(field, at, up):
        return pltpu.make_async_remote_copy(
            src_ref=field.at[:, pl.ds(axial if up else 1, 1), cells, :],
            dst_ref=field.at[:, pl.ds(0 if up else axial + 1, 1), cells, :],
            send_sem=ax_send.at[at],
            recv_sem=ax_recv.at[at],
            device_id=(region, slab + 1 if up else slab - 1),
            device_id_type=MESH,
        )

    up_copies = [axial_copy(b_s, 0, True), axial_copy(u_s, 1, True)]
    down_copies = [axial_copy(b_s, 2, False), axial_copy(u_s, 3, False)]

    lane = iota((radial, LANES), 1)
    pair = lax.rem(lane + 1, LANES) // 2

    for f, field in enumerate((b_s, u_s)):
        def pack(z, total, field=field):
            for c in range(3):
                at = c * axial + z
                plane = field[c, z + 1, PAD : PAD + radial, :]
                total = jnp.where(pair == at, pltpu.roll(plane, 2 * at, 1), total)
                field[c, z + 1, PAD - 1 : PAD, :] = plane[0:1]
                field[c, z + 1, PAD + radial : PAD + radial + 1, :] = plane[radial - 1 : radial]
            return total

        pack_s[f] = lax.fori_loop(0, axial, pack, jnp.zeros((radial, LANES), F32))

    left = lax.rem(region + regions - 1, regions)
    right = lax.rem(region + 1, regions)

    def azimuth_copy(at, target):
        return pltpu.make_async_remote_copy(
            src_ref=pack_s,
            dst_ref=around_s.at[at],
            send_sem=az_send.at[at],
            recv_sem=az_recv.at[at],
            device_id=(target, slab),
            device_id_type=MESH,
        )

    azimuth_copies = [azimuth_copy(0, right)]
    if regions > 2:
        azimuth_copies.append(azimuth_copy(1, left))
    for copy in azimuth_copies:
        copy.start()

    @pl.when(slab < slabs - 1)
    def _():
        for copy in up_copies:
            copy.start()

    @pl.when(slab > 0)
    def _():
        for copy in down_copies:
            copy.start()

    @pl.when(slab == 0)
    def _():
        for field in (b_s, u_s):
            field[:, 0, PAD : PAD + radial, :] = jnp.zeros((3, radial, LANES), F32)

    @pl.when(slab == slabs - 1)
    def _():
        for field in (b_s, u_s):
            field[:, axial + 1, PAD : PAD + radial, :] = jnp.zeros((3, radial, LANES), F32)

    load_w.wait()
    for s in range(mode_count):
        whi_s[s], wlo_s[s] = split(wall_s[s])

    def wait_all(buffer, sem):
        part = buffer.at[pl.ds(0, count - 1)]
        pltpu.make_async_copy(part, part, sem).wait()

    wait_all(recv1, a2a_recv.at[0])
    shape = (axial, LANES)
    own_cell = lax.rem(iota(shape, 1), axial) == iota(shape, 0)
    for j in range(slabs):
        got = recv1[j]
        for g in range(1, regions):
            got = got + recv1[g * slabs + j]
        for r in range(rows_each):
            hi, lo = split(jnp.where(own_cell, got[r : r + 1], 0.0))
            spread_s[r, 0, axial * j : axial * (j + 1), :] = hi
            spread_s[r, 1, axial * j : axial * (j + 1), :] = lo
    shape = (LANES, LANES)
    group = jnp.where(iota(shape, 0) // axial == iota(shape, 1) // axial, 1.0, 0.0).astype(BF16)
    shape = (nz, LANES)
    own_lane = lax.rem(iota(shape, 1), axial) == lax.rem(iota(shape, 0), axial)
    lane_group = iota(shape, 1) // (2 * axial)
    for r in range(rows_each):
        hi = jnp.dot(spread_s[r, 0], group, preferred_element_type=F32).astype(BF16)
        lo = jnp.dot(spread_s[r, 1], group, preferred_element_type=F32).astype(BF16)
        both = jnp.concatenate([hi, lo], axis=1)
        total = jnp.zeros((nz, LANES), F32)
        for q in range(per_row):
            s = r * per_row + q
            first = jnp.dot(whi_s[s], both, preferred_element_type=F32)
            second = jnp.dot(wlo_s[s], hi, preferred_element_type=F32)
            answer = first[:, :LANES] + (first[:, LANES:] + second)
            total = jnp.where(own_lane & (lane_group == q), answer, total)
        message = jnp.sum(total.reshape(slabs, axial, LANES), axis=1)
        for j in range(slabs):
            send2[j, r : r + 1, :] = message[j : j + 1]
    recv2[pl.ds(me, 1)] = send2[pl.ds(slab, 1)]

    @pl.loop(1, count)
    def _(i):
        other = lax.rem(me + i, count)
        target = lax.rem(other, slabs)
        pltpu.make_async_remote_copy(
            src_ref=send2.at[target],
            dst_ref=recv2.at[me],
            send_sem=a2a_send.at[1],
            recv_sem=a2a_recv.at[1],
            device_id=(other // slabs, target),
            device_id_type=MESH,
        ).start()

    for copy in azimuth_copies:
        copy.wait()

    even = lax.rem(lane, 2) == 0
    for f in range(2):
        from_left = around_s[0, f]
        from_right = around_s[len(azimuth_copies) - 1, f]
        halo_s[f] = jnp.where(
            even, pltpu.roll(from_left, 1, 1), pltpu.roll(from_right, LANES - 1, 1)
        )

    @pl.when(slab < slabs - 1)
    def _():
        for copy in up_copies:
            copy.wait_send()
        for copy in down_copies:
            copy.wait_recv()

    @pl.when(slab > 0)
    def _():
        for copy in down_copies:
            copy.wait_send()
        for copy in up_copies:
            copy.wait_recv()

    depth = 16
    first_lane = iota((depth, LANES), 1) == 0
    last_lane = iota((depth, LANES), 1) == LANES - 1

    def advance(z, carry):
        for start in range(0, radial, depth):
            rows = slice(PAD + start, PAD + start + depth)
            above = slice(PAD + start + 1, PAD + start + depth + 1)
            below = slice(PAD + start - 1, PAD + start + depth - 1)
            here = slice(start, start + depth)
            ap = radial_s[0, here, :]
            kp = radial_s[1, here, :]
            k1 = radial_s[2, here, :]
            kc = radial_s[3, here, :]

            def around(f, c, center):
                shift = lax.rem(LANES - lax.rem(2 * (c * axial + z), LANES), LANES)
                halo = pltpu.roll(halo_s[f, here, :], shift, 1)
                before = jnp.where(first_lane, halo, pltpu.roll(center, 1, 1))
                after = jnp.where(last_lane, halo, pltpu.roll(center, LANES - 1, 1))
                return before, after

            b = [b_s[c, z + 1, rows, :] for c in range(3)]
            u = [u_s[c, z + 1, rows, :] for c in range(3)]
            ur, up, uz = ar * u[0] - k1, ap * u[1], az * u[2]
            br, bp, bz = ar * b[0], ap * b[1], az * b[2]
            r_next, r_last = kr - ur, kr + ur
            p_next, p_last = kp - up, kp + up
            z_next, z_last = kz - uz, kz + uz
            for c in range(3):
                before, after = around(0, c, b[c])
                value = b[c] * kc
                value += r_next * b_s[c, z + 1, above, :] + r_last * b_s[c, z + 1, below, :]
                value += p_next * after + p_last * before
                value += z_next * b_s[c, z + 2, rows, :] + z_last * b_s[c, z, rows, :]
                before, after = around(1, c, u[c])
                value += br * (u_s[c, z + 1, above, :] - u_s[c, z + 1, below, :])
                value += bp * (after - before)
                value += bz * (u_s[c, z + 2, rows, :] - u_s[c, z, rows, :])
                out_s[c, z, here, :] = value
        return carry

    lax.fori_loop(0, axial, advance, 0)
    top = radial - 8
    store_inner = pltpu.make_async_copy(
        out_s.at[:, :, 0:top, :], next_hbm.at[:, :, 0:top, :], store_sem.at[0]
    )
    store_inner.start()

    for z in range(axial):
        trace_s[z : z + 1, :] = u_s[0, z + 1, PAD + radial - 1 : PAD + radial, :]
    outer = kr + radial_s[2, radial - 1 : radial, :] - ar * trace_s[0:axial, :]
    thickness = layer_ref[...].astype(F32) * (1.0 / LW)
    wait_all(recv2, a2a_recv.at[1])
    for o in range(count):
        row_s[rows_each * o : rows_each * (o + 1), :] = recv2[o]
    turned = row_s[...].T
    flux = jnp.zeros((2 * axial, LANES), F32)
    for q in range(per_row):
        flux += exact_dot(
            turned[2 * axial * q : 2 * axial * (q + 1)],
            weighted_s[:, LANES * q : LANES * (q + 1)],
            ((1,), (0,)),
        )
    flux_ref[...] = flux
    change = flux * thickness * jnp.concatenate([outer, outer], axis=0)
    for c in range(2):
        for z in range(axial):
            at = c * axial + z
            out_s[c + 1, z, radial - 1 : radial, :] = (
                out_s[c + 1, z, radial - 1 : radial, :] - change[at : at + 1]
            )
    store_outer = pltpu.make_async_copy(
        out_s.at[:, :, top:radial, :], next_hbm.at[:, :, top:radial, :], store_sem.at[1]
    )
    store_outer.start()
    wait_all(recv1, a2a_send.at[0])
    wait_all(recv2, a2a_send.at[1])
    store_inner.wait()
    store_outer.wait()


def solution(mesh):
    regions = mesh.shape["region"]
    slabs = mesh.shape["slab"]
    count = regions * slabs

    def shards(magnetic, velocity, wall_response, mode_slots, wall_layers):
        _, axial, radial, azimuth = magnetic.shape
        azimuth_total = mode_slots.shape[0]
        mode_count, nz, _ = wall_response.shape
        rows_each = mode_count * 2 * axial // LANES
        per_row = LANES // (2 * axial)
        padded = max(LANES, count * rows_each)
        vmem = pl.BlockSpec(memory_space=pltpu.VMEM)
        hbm = pl.BlockSpec(memory_space=pl.ANY)
        field = pltpu.VMEM((3, axial + 2, radial + 2 * PAD, azimuth), F32)
        magnetic_next, flux = pl.pallas_call(
            functools.partial(step_kernel, regions, slabs),
            out_shape=(
                jax.ShapeDtypeStruct(magnetic.shape, F32),
                jax.ShapeDtypeStruct((2 * axial, azimuth), F32),
            ),
            in_specs=[vmem, vmem, hbm, hbm, hbm],
            out_specs=(hbm, vmem),
            scratch_shapes=[
                field,
                field,
                pltpu.VMEM(magnetic.shape, F32),
                pltpu.VMEM(wall_response.shape, F32),
                pltpu.VMEM(wall_response.shape, BF16),
                pltpu.VMEM(wall_response.shape, BF16),
                pltpu.VMEM((padded, per_row * LANES), F32),
                pltpu.VMEM((padded, per_row * LANES), F32),
                pltpu.VMEM((2 * axial, LANES), F32),
                pltpu.VMEM((LANES, per_row * LANES), F32),
                pltpu.VMEM((4, radial, LANES), F32),
                pltpu.VMEM((padded, LANES), F32),
                pltpu.VMEM((rows_each, 2, nz, LANES), BF16),
                pltpu.VMEM((count, rows_each, LANES), F32),
                pltpu.VMEM((count, rows_each, LANES), F32),
                pltpu.VMEM((slabs, rows_each, LANES), F32),
                pltpu.VMEM((count, rows_each, LANES), F32),
                pltpu.VMEM((2, radial, LANES), F32),
                pltpu.VMEM((2, 2, radial, LANES), F32),
                pltpu.VMEM((2, radial, LANES), F32),
                pltpu.SemaphoreType.DMA((3,)),
                pltpu.SemaphoreType.DMA((2,)),
                pltpu.SemaphoreType.DMA((2,)),
                pltpu.SemaphoreType.DMA((2,)),
                pltpu.SemaphoreType.DMA((4,)),
                pltpu.SemaphoreType.DMA((4,)),
                pltpu.SemaphoreType.DMA((2,)),
                pltpu.SemaphoreType.DMA((2,)),
            ],
            compiler_params=pltpu.CompilerParams(
                collective_id=0, has_side_effects=True, vmem_limit_bytes=48 * 1024 * 1024
            ),
            name="wall_step",
        )(
            mode_slots.reshape(1, azimuth_total),
            wall_layers.reshape(1, azimuth),
            magnetic,
            velocity,
            wall_response,
        )
        return magnetic_next, flux.reshape(2, axial, azimuth)

    placed = (
        P(None, "slab", None, "region"),
        P(None, "slab", None, "region"),
        P(("region", "slab"), None, None),
        P(),
        P("region"),
    )
    return jax.shard_map(
        shards,
        mesh=mesh,
        in_specs=placed,
        out_specs=(P(None, "slab", None, "region"), P(None, "slab", "region")),
        check_vma=False,
    )
```

```python
import functools
import math

import jax
import jax.numpy as jnp
from jax import lax
from jax.experimental import pallas as pl
from jax.experimental.pallas import tpu as pltpu
from jax.sharding import PartitionSpec as P

LW = 8
TIME_STEP = 0.0003
DIFFUSIVITY = 0.001
RADIAL_STEP = 1.0 / 384.0
AXIAL_STEP = 1.0 / 768.0
MESH = pl.DeviceIdType.MESH
F32 = jnp.float32
BF16 = jnp.bfloat16

PAD = 8
LANES = 128


def iota(shape, dim):
    return lax.broadcasted_iota(jnp.int32, shape, dim)


def split(x):
    hi = x.astype(BF16)
    return hi, (x - hi.astype(F32)).astype(BF16)


def sine(t):
    s = t * t
    value = 1.0 / math.factorial(13)
    for n in (11, 9, 7, 5, 3, 1):
        sign = 1.0 if (n // 2) % 2 == 0 else -1.0
        value = value * s + sign / math.factorial(n)
    return value * t


def step_kernel(
    regions,
    slabs,
    mode_ref,
    layer_ref,
    mag_hbm,
    vel_hbm,
    wall_hbm,
    out_s,
    row_s,
    weight_hi,
    weight_lo,
    outer_s,
    b_s,
    u_s,
    mode_s,
    layer_s,
    wall_s,
    whi_s,
    wlo_s,
    trace_s,
    block_hi,
    block_lo,
    radial_s,
    spread_s,
    send1,
    recv1,
    send2,
    recv2,
    pack_s,
    around_s,
    halo_s,
    load_sem,
    a2a_send,
    a2a_recv,
    ax_send,
    ax_recv,
    az_send,
    az_recv,
):
    count = regions * slabs
    radial = mag_hbm.shape[2]
    axial = mag_hbm.shape[1]
    azimuth_total = mode_s.shape[1]
    mode_count, nz, _ = wall_hbm.shape
    rows_each = send1.shape[1]
    slot_rows = count * rows_each
    per_row = LANES // (2 * axial)
    region = lax.axis_index("region")
    slab = lax.axis_index("slab")
    me = region * slabs + slab
    cells = pl.ds(PAD, radial)

    load_b = pltpu.make_async_copy(mag_hbm, b_s.at[:, 1 : axial + 1, cells, :], load_sem.at[0])
    load_u = pltpu.make_async_copy(vel_hbm, u_s.at[:, 1 : axial + 1, cells, :], load_sem.at[1])
    load_w = pltpu.make_async_copy(wall_hbm, wall_s, load_sem.at[2])
    load_modes = pltpu.make_async_copy(mode_ref, mode_s, load_sem.at[3])
    load_layers = pltpu.make_async_copy(layer_ref, layer_s, load_sem.at[4])
    load_modes.start()
    load_b.start()
    load_u.start()
    load_layers.start()
    load_w.start()

    barrier = pltpu.get_barrier_semaphore()

    @pl.loop(1, count)
    def _(i):
        other = lax.rem(me + i, count)
        pl.semaphore_signal(
            barrier,
            inc=1,
            device_id=(other // slabs, lax.rem(other, slabs)),
            device_id_type=MESH,
        )

    block_hi[...] = jnp.zeros(block_hi.shape, BF16)
    block_lo[...] = jnp.zeros(block_lo.shape, BF16)
    shape = (azimuth_total, per_row * LANES)
    picks = jnp.where(lax.rem(iota(shape, 0), per_row) == iota(shape, 1) // LANES, 1.0, 0.0)
    shape = (slot_rows, azimuth_total)
    mine = iota(shape, 1) // per_row == iota(shape, 0)
    load_modes.wait()
    modes = mode_s[...].astype(F32)
    tens = jnp.floor(modes * (1.0 / 32.0))
    parts = [jnp.where(mine, part, 0.0) for part in (tens, modes - 32.0 * tens)]
    parts = jnp.dot(
        jnp.concatenate(parts, axis=0).astype(BF16),
        picks.astype(BF16),
        preferred_element_type=F32,
    )
    mode = 32.0 * parts[:slot_rows] + parts[slot_rows:]
    half = jnp.floor(mode * 0.5)
    odd = mode - 2.0 * half
    cell = region * LANES + lax.rem(iota(mode.shape, 1), LANES)
    turn = (half + odd) * (2 * cell + 1).astype(F32) - odd * (azimuth_total // 2)
    turn = turn * (0.5 / azimuth_total)
    turn = turn - jnp.floor(turn + 0.5)
    table = sine((0.25 - jnp.abs(turn)) * (2.0 * math.pi))
    table_hi, table_lo = split(table)

    load_b.wait()
    for c in range(2):
        for z in range(axial):
            at = c * axial + z
            trace_s[at : at + 1, :] = b_s[c + 1, z + 1, PAD + radial - 1 : PAD + radial, :]
    trace_hi, trace_lo = split(trace_s[...])
    for q in range(per_row):
        block_hi[2 * axial * q : 2 * axial * (q + 1), LANES * q : LANES * (q + 1)] = trace_hi
        block_lo[2 * axial * q : 2 * axial * (q + 1), LANES * q : LANES * (q + 1)] = trace_lo
    both = jnp.concatenate([table_hi, table_lo], axis=0)
    turned = (((1,), (1,)), ((), ()))
    first = lax.dot_general(both, block_hi[...], turned, preferred_element_type=F32)
    second = lax.dot_general(table_hi, block_lo[...], turned, preferred_element_type=F32)
    coefficients = first[:slot_rows] + (first[slot_rows:] + second)
    for o in range(count):
        send1[o] = coefficients[rows_each * o : rows_each * (o + 1)]
    recv1[pl.ds(me, 1)] = send1[pl.ds(me, 1)]

    pl.semaphore_wait(barrier, count - 1)

    @pl.loop(1, count)
    def _(i):
        other = lax.rem(me + i, count)
        pltpu.make_async_remote_copy(
            src_ref=send1.at[other],
            dst_ref=recv1.at[me],
            send_sem=a2a_send.at[0],
            recv_sem=a2a_recv.at[0],
            device_id=(other // slabs, lax.rem(other, slabs)),
            device_id_type=MESH,
        ).start()

    single = (mode == 0.0) | (mode == azimuth_total - 1.0)
    weight_hi[...], weight_lo[...] = split(table * (jnp.where(single, 1.0, 2.0) / azimuth_total))

    shape = (radial, LANES)
    radius = 1.0 - (radial - iota(shape, 0).astype(F32) - 0.5) * RADIAL_STEP
    inverse = 1.0 / radius
    angle_step = 2.0 * math.pi / azimuth_total
    kr = TIME_STEP * DIFFUSIVITY / RADIAL_STEP**2
    kz = TIME_STEP * DIFFUSIVITY / AXIAL_STEP**2
    ar = TIME_STEP / (2.0 * RADIAL_STEP)
    az = TIME_STEP / (2.0 * AXIAL_STEP)
    kp = inverse * inverse * (TIME_STEP * DIFFUSIVITY / angle_step**2)
    radial_s[0] = inverse * (TIME_STEP / (2.0 * angle_step))
    radial_s[1] = kp
    radial_s[2] = inverse * (TIME_STEP * DIFFUSIVITY / (2.0 * RADIAL_STEP))
    radial_s[3] = (1.0 - 2.0 * kr - 2.0 * kz) - 2.0 * kp

    load_u.wait()

    def axial_copy(field, at, up):
        return pltpu.make_async_remote_copy(
            src_ref=field.at[:, pl.ds(axial if up else 1, 1), cells, :],
            dst_ref=field.at[:, pl.ds(0 if up else axial + 1, 1), cells, :],
            send_sem=ax_send.at[at],
            recv_sem=ax_recv.at[at],
            device_id=(region, slab + 1 if up else slab - 1),
            device_id_type=MESH,
        )

    up_copies = [axial_copy(b_s, 0, True), axial_copy(u_s, 1, True)]
    down_copies = [axial_copy(b_s, 2, False), axial_copy(u_s, 3, False)]

    lane = iota((radial, LANES), 1)
    pair = lax.rem(lane + 1, LANES) // 2

    for f, field in enumerate((b_s, u_s)):
        def pack(z, total, field=field):
            for c in range(3):
                at = c * axial + z
                plane = field[c, z + 1, PAD : PAD + radial, :]
                total = jnp.where(pair == at, pltpu.roll(plane, 2 * at, 1), total)
                field[c, z + 1, PAD - 1 : PAD, :] = plane[0:1]
                field[c, z + 1, PAD + radial : PAD + radial + 1, :] = plane[radial - 1 : radial]
            return total

        pack_s[f] = lax.fori_loop(0, axial, pack, jnp.zeros((radial, LANES), F32))

    left = lax.rem(region + regions - 1, regions)
    right = lax.rem(region + 1, regions)

    def azimuth_copy(at, target):
        return pltpu.make_async_remote_copy(
            src_ref=pack_s,
            dst_ref=around_s.at[at],
            send_sem=az_send.at[at],
            recv_sem=az_recv.at[at],
            device_id=(target, slab),
            device_id_type=MESH,
        )

    azimuth_copies = [azimuth_copy(0, right)]
    if regions > 2:
        azimuth_copies.append(azimuth_copy(1, left))
    for copy in azimuth_copies:
        copy.start()

    @pl.when(slab < slabs - 1)
    def _():
        for copy in up_copies:
            copy.start()

    @pl.when(slab > 0)
    def _():
        for copy in down_copies:
            copy.start()

    @pl.when(slab == 0)
    def _():
        for field in (b_s, u_s):
            field[:, 0, PAD : PAD + radial, :] = jnp.zeros((3, radial, LANES), F32)

    @pl.when(slab == slabs - 1)
    def _():
        for field in (b_s, u_s):
            field[:, axial + 1, PAD : PAD + radial, :] = jnp.zeros((3, radial, LANES), F32)

    load_w.wait()
    for s in range(mode_count):
        whi_s[s], wlo_s[s] = split(wall_s[s])

    def wait_all(buffer, sem):
        part = buffer.at[pl.ds(0, count - 1)]
        pltpu.make_async_copy(part, part, sem).wait()

    wait_all(recv1, a2a_recv.at[0])
    shape = (axial, LANES)
    own_cell = lax.rem(iota(shape, 1), axial) == iota(shape, 0)
    for j in range(slabs):
        got = recv1[j]
        for g in range(1, regions):
            got = got + recv1[g * slabs + j]
        for r in range(rows_each):
            hi, lo = split(jnp.where(own_cell, got[r : r + 1], 0.0))
            spread_s[r, 0, axial * j : axial * (j + 1), :] = hi
            spread_s[r, 1, axial * j : axial * (j + 1), :] = lo
    shape = (LANES, LANES)
    group = jnp.where(iota(shape, 0) // axial == iota(shape, 1) // axial, 1.0, 0.0).astype(BF16)
    shape = (nz, LANES)
    own_lane = lax.rem(iota(shape, 1), axial) == lax.rem(iota(shape, 0), axial)
    lane_group = iota(shape, 1) // (2 * axial)
    for r in range(rows_each):
        hi = jnp.dot(spread_s[r, 0], group, preferred_element_type=F32).astype(BF16)
        lo = jnp.dot(spread_s[r, 1], group, preferred_element_type=F32).astype(BF16)
        both = jnp.concatenate([hi, lo], axis=1)
        total = jnp.zeros((nz, LANES), F32)
        for q in range(per_row):
            s = r * per_row + q
            first = jnp.dot(whi_s[s], both, preferred_element_type=F32)
            second = jnp.dot(wlo_s[s], hi, preferred_element_type=F32)
            answer = first[:, :LANES] + (first[:, LANES:] + second)
            total = jnp.where(own_lane & (lane_group == q), answer, total)
        message = jnp.sum(total.reshape(slabs, axial, LANES), axis=1)
        for j in range(slabs):
            send2[j, r : r + 1, :] = message[j : j + 1]
    recv2[pl.ds(me, 1)] = send2[pl.ds(slab, 1)]

    @pl.loop(1, count)
    def _(i):
        other = lax.rem(me + i, count)
        target = lax.rem(other, slabs)
        pltpu.make_async_remote_copy(
            src_ref=send2.at[target],
            dst_ref=recv2.at[me],
            send_sem=a2a_send.at[1],
            recv_sem=a2a_recv.at[1],
            device_id=(other // slabs, target),
            device_id_type=MESH,
        ).start()

    for copy in azimuth_copies:
        copy.wait()

    even = lax.rem(lane, 2) == 0
    for f in range(2):
        from_left = around_s[0, f]
        from_right = around_s[len(azimuth_copies) - 1, f]
        halo_s[f] = jnp.where(
            even, pltpu.roll(from_left, 1, 1), pltpu.roll(from_right, LANES - 1, 1)
        )

    @pl.when(slab < slabs - 1)
    def _():
        for copy in up_copies:
            copy.wait_send()
        for copy in down_copies:
            copy.wait_recv()

    @pl.when(slab > 0)
    def _():
        for copy in down_copies:
            copy.wait_send()
        for copy in up_copies:
            copy.wait_recv()

    depth = 16
    first_lane = iota((depth, LANES), 1) == 0
    last_lane = iota((depth, LANES), 1) == LANES - 1

    def advance(z, carry):
        for start in range(0, radial, depth):
            rows = slice(PAD + start, PAD + start + depth)
            above = slice(PAD + start + 1, PAD + start + depth + 1)
            below = slice(PAD + start - 1, PAD + start + depth - 1)
            here = slice(start, start + depth)
            ap = radial_s[0, here, :]
            kp = radial_s[1, here, :]
            k1 = radial_s[2, here, :]
            kc = radial_s[3, here, :]

            def around(f, c, center):
                shift = lax.rem(LANES - lax.rem(2 * (c * axial + z), LANES), LANES)
                halo = pltpu.roll(halo_s[f, here, :], shift, 1)
                before = jnp.where(first_lane, halo, pltpu.roll(center, 1, 1))
                after = jnp.where(last_lane, halo, pltpu.roll(center, LANES - 1, 1))
                return before, after

            b = [b_s[c, z + 1, rows, :] for c in range(3)]
            u = [u_s[c, z + 1, rows, :] for c in range(3)]
            ur, up, uz = ar * u[0] - k1, ap * u[1], az * u[2]
            br, bp, bz = ar * b[0], ap * b[1], az * b[2]
            r_next, r_last = kr - ur, kr + ur
            p_next, p_last = kp - up, kp + up
            z_next, z_last = kz - uz, kz + uz
            for c in range(3):
                before, after = around(0, c, b[c])
                value = b[c] * kc
                value += r_next * b_s[c, z + 1, above, :] + r_last * b_s[c, z + 1, below, :]
                value += p_next * after + p_last * before
                value += z_next * b_s[c, z + 2, rows, :] + z_last * b_s[c, z, rows, :]
                before, after = around(1, c, u[c])
                value += br * (u_s[c, z + 1, above, :] - u_s[c, z + 1, below, :])
                value += bp * (after - before)
                value += bz * (u_s[c, z + 2, rows, :] - u_s[c, z, rows, :])
                out_s[c, z, here, :] = value
        return carry

    lax.fori_loop(0, axial, advance, 0)
    load_layers.wait()
    for z in range(axial):
        trace_s[z : z + 1, :] = u_s[0, z + 1, PAD + radial - 1 : PAD + radial, :]
    outer = kr + radial_s[2, radial - 1 : radial, :] - ar * trace_s[0:axial, :]
    outer_s[...] = outer * (layer_s[...].astype(F32) * (1.0 / LW))
    wait_all(recv2, a2a_recv.at[1])
    for o in range(count):
        row_s[rows_each * o : rows_each * (o + 1), :] = recv2[o]
    wait_all(recv1, a2a_send.at[0])
    wait_all(recv2, a2a_send.at[1])


def finish_kernel(
    out_ref, row_ref, weight_hi, weight_lo, outer_ref, next_hbm, flux_hbm, edge_s, flux_s, sem
):
    _, axial, radial, _ = out_ref.shape
    top = radial - 8
    inner = pltpu.make_async_copy(
        out_ref.at[:, :, 0:top, :], next_hbm.at[:, :, 0:top, :], sem.at[0]
    )
    inner.start()
    hi, lo = split(row_ref[...].T)
    flux = jnp.zeros((2 * axial, LANES), F32)
    for q in range(LANES // (2 * axial)):
        part = slice(2 * axial * q, 2 * axial * (q + 1))
        lanes = slice(LANES * q, LANES * (q + 1))
        flux += jnp.dot(hi[part], weight_hi[:, lanes], preferred_element_type=F32)
        flux += jnp.dot(lo[part], weight_hi[:, lanes], preferred_element_type=F32)
        flux += jnp.dot(hi[part], weight_lo[:, lanes], preferred_element_type=F32)
    flux_s[...] = flux
    store_flux = pltpu.make_async_copy(flux_s, flux_hbm, sem.at[1])
    store_flux.start()
    outer = outer_ref[...]
    last = iota((8, LANES), 0) == 7
    for z in range(axial):
        edge_s[0, z] = out_ref[0, z, top:radial, :]
    for c in range(2):
        change = flux[axial * c : axial * (c + 1)] * outer
        for z in range(axial):
            edge = out_ref[c + 1, z, top:radial, :]
            edge_s[c + 1, z] = jnp.where(last, edge - change[z : z + 1], edge)
    store_edge = pltpu.make_async_copy(edge_s, next_hbm.at[:, :, top:radial, :], sem.at[2])
    store_edge.start()
    inner.wait()
    store_flux.wait()
    store_edge.wait()


def solution(mesh):
    regions = mesh.shape["region"]
    slabs = mesh.shape["slab"]
    count = regions * slabs

    def shards(magnetic, velocity, wall_response, mode_slots, wall_layers):
        _, axial, radial, azimuth = magnetic.shape
        azimuth_total = mode_slots.shape[0]
        mode_count, nz, _ = wall_response.shape
        rows_each = mode_count * 2 * axial // LANES
        per_row = LANES // (2 * axial)
        slot_rows = count * rows_each
        vmem = pl.BlockSpec(memory_space=pltpu.VMEM)
        hbm = pl.BlockSpec(memory_space=pltpu.HBM)
        field = pltpu.VMEM((3, axial + 2, radial + 2 * PAD, azimuth), F32)
        kept = pl.pallas_call(
            functools.partial(step_kernel, regions, slabs),
            out_shape=(
                pltpu.VMEM(magnetic.shape, F32),
                pltpu.VMEM((slot_rows, LANES), F32),
                pltpu.VMEM((slot_rows, per_row * LANES), BF16),
                pltpu.VMEM((slot_rows, per_row * LANES), BF16),
                pltpu.VMEM((axial, LANES), F32),
            ),
            in_specs=[hbm] * 5,
            out_specs=(vmem,) * 5,
            scratch_shapes=[
                field,
                field,
                pltpu.VMEM((1, azimuth_total), jnp.int32),
                pltpu.VMEM((1, azimuth), jnp.int32),
                pltpu.VMEM(wall_response.shape, F32),
                pltpu.VMEM(wall_response.shape, BF16),
                pltpu.VMEM(wall_response.shape, BF16),
                pltpu.VMEM((2 * axial, LANES), F32),
                pltpu.VMEM((LANES, per_row * LANES), BF16),
                pltpu.VMEM((LANES, per_row * LANES), BF16),
                pltpu.VMEM((4, radial, LANES), F32),
                pltpu.VMEM((rows_each, 2, nz, LANES), BF16),
                pltpu.VMEM((count, rows_each, LANES), F32),
                pltpu.VMEM((count, rows_each, LANES), F32),
                pltpu.VMEM((slabs, rows_each, LANES), F32),
                pltpu.VMEM((count, rows_each, LANES), F32),
                pltpu.VMEM((2, radial, LANES), F32),
                pltpu.VMEM((2, 2, radial, LANES), F32),
                pltpu.VMEM((2, radial, LANES), F32),
                pltpu.SemaphoreType.DMA((5,)),
                pltpu.SemaphoreType.DMA((2,)),
                pltpu.SemaphoreType.DMA((2,)),
                pltpu.SemaphoreType.DMA((4,)),
                pltpu.SemaphoreType.DMA((4,)),
                pltpu.SemaphoreType.DMA((2,)),
                pltpu.SemaphoreType.DMA((2,)),
            ],
            compiler_params=pltpu.CompilerParams(
                collective_id=0, has_side_effects=True, vmem_limit_bytes=48 * 1024 * 1024
            ),
            name="wall_step",
        )(
            *(
                pltpu.with_memory_space_constraint(x, pltpu.HBM)
                for x in (
                    mode_slots.reshape(1, azimuth_total),
                    wall_layers.reshape(1, azimuth),
                    magnetic,
                    velocity,
                    wall_response,
                )
            )
        )
        magnetic_next, flux = pl.pallas_call(
            finish_kernel,
            out_shape=(
                jax.ShapeDtypeStruct(magnetic.shape, F32),
                jax.ShapeDtypeStruct((2 * axial, azimuth), F32),
            ),
            in_specs=[vmem] * 5,
            out_specs=(hbm, hbm),
            scratch_shapes=[
                pltpu.VMEM((3, axial, 8, LANES), F32),
                pltpu.VMEM((2 * axial, LANES), F32),
                pltpu.SemaphoreType.DMA((3,)),
            ],
            compiler_params=pltpu.CompilerParams(vmem_limit_bytes=48 * 1024 * 1024),
            name="wall_finish",
        )(*(pltpu.with_memory_space_constraint(x, pltpu.VMEM) for x in kept))
        return magnetic_next, flux.reshape(2, axial, azimuth)

    placed = (
        P(None, "slab", None, "region"),
        P(None, "slab", None, "region"),
        P(("region", "slab"), None, None),
        P(),
        P("region"),
    )
    return jax.shard_map(
        shards,
        mesh=mesh,
        in_specs=placed,
        out_specs=(P(None, "slab", None, "region"), P(None, "slab", "region")),
        check_vma=False,
    )
```

```python
import functools
import math

import jax
import jax.numpy as jnp
from jax import lax
from jax.experimental import pallas as pl
from jax.experimental.pallas import tpu as pltpu
from jax.sharding import PartitionSpec as P

LW = 8
TIME_STEP = 0.0003
DIFFUSIVITY = 0.001
RADIAL_STEP = 1.0 / 384.0
AXIAL_STEP = 1.0 / 768.0
MESH = pl.DeviceIdType.MESH
F32 = jnp.float32
BF16 = jnp.bfloat16

PAD = 8
LANES = 128


def iota(shape, dim):
    return lax.broadcasted_iota(jnp.int32, shape, dim)


def split(x):
    hi = x.astype(BF16)
    return hi, (x - hi.astype(F32)).astype(BF16)


def sine(t):
    s = t * t
    value = 1.0 / math.factorial(13)
    for n in (11, 9, 7, 5, 3, 1):
        sign = 1.0 if (n // 2) % 2 == 0 else -1.0
        value = value * s + sign / math.factorial(n)
    return value * t


def step_kernel(
    regions,
    slabs,
    mode_ref,
    layer_ref,
    mag_hbm,
    vel_hbm,
    wall_hbm,
    out_s,
    row_s,
    weight_hi,
    weight_lo,
    outer_s,
    b_s,
    u_s,
    mode_s,
    layer_s,
    wall_s,
    whi_s,
    wlo_s,
    edge_s,
    trace_s,
    block_hi,
    block_lo,
    radial_s,
    spread_s,
    send1,
    recv1,
    send2,
    recv2,
    pack_s,
    around_s,
    halo_s,
    load_sem,
    a2a_send,
    a2a_recv,
    ax_send,
    ax_recv,
    az_send,
    az_recv,
):
    count = regions * slabs
    radial = mag_hbm.shape[2]
    axial = mag_hbm.shape[1]
    azimuth_total = mode_s.shape[1]
    mode_count, nz, _ = wall_hbm.shape
    rows_each = send1.shape[1]
    slot_rows = count * rows_each
    per_row = LANES // (2 * axial)
    region = lax.axis_index("region")
    slab = lax.axis_index("slab")
    me = region * slabs + slab
    cells = pl.ds(PAD, radial)

    load_b = pltpu.make_async_copy(mag_hbm, b_s.at[:, 1 : axial + 1, cells, :], load_sem.at[0])
    load_u = pltpu.make_async_copy(vel_hbm, u_s.at[:, 1 : axial + 1, cells, :], load_sem.at[1])
    load_w = pltpu.make_async_copy(wall_hbm, wall_s, load_sem.at[2])
    load_modes = pltpu.make_async_copy(mode_ref, mode_s, load_sem.at[3])
    load_layers = pltpu.make_async_copy(layer_ref, layer_s, load_sem.at[4])
    load_trace = pltpu.make_async_copy(
        mag_hbm.at[1:3, :, radial - 8 : radial, :], edge_s, load_sem.at[5]
    )
    load_modes.start()
    load_trace.start()
    load_b.start()
    load_u.start()
    load_layers.start()
    load_w.start()

    barrier = pltpu.get_barrier_semaphore()

    def each_other(act):
        for step in range(regions):
            its_region = lax.rem(region + step, regions)

            @pl.loop(0 if step else 1, slabs)
            def _(i, its_region=its_region):
                act(its_region, lax.rem(slab + i, slabs))

    def greet(its_region, its_slab):
        pl.semaphore_signal(
            barrier, inc=1, device_id=(its_region, its_slab), device_id_type=MESH
        )

    each_other(greet)

    block_hi[...] = jnp.zeros(block_hi.shape, BF16)
    block_lo[...] = jnp.zeros(block_lo.shape, BF16)
    shape = (azimuth_total, per_row * LANES)
    picks = jnp.where(lax.rem(iota(shape, 0), per_row) == iota(shape, 1) // LANES, 1.0, 0.0)
    shape = (slot_rows, azimuth_total)
    mine = iota(shape, 1) // per_row == iota(shape, 0)
    load_modes.wait()
    modes = mode_s[...].astype(F32)
    tens = jnp.floor(modes * (1.0 / 32.0))
    parts = [jnp.where(mine, part, 0.0) for part in (tens, modes - 32.0 * tens)]
    parts = jnp.dot(
        jnp.concatenate(parts, axis=0).astype(BF16),
        picks.astype(BF16),
        preferred_element_type=F32,
    )
    mode = 32.0 * parts[:slot_rows] + parts[slot_rows:]
    half = jnp.floor(mode * 0.5)
    odd = mode - 2.0 * half
    cell = region * LANES + lax.rem(iota(mode.shape, 1), LANES)
    turn = (half + odd) * (2 * cell + 1).astype(F32) - odd * (azimuth_total // 2)
    turn = turn * (0.5 / azimuth_total)
    turn = turn - jnp.floor(turn + 0.5)
    table = sine((0.25 - jnp.abs(turn)) * (2.0 * math.pi))
    table_hi, table_lo = split(table)

    load_trace.wait()
    for c in range(2):
        for z in range(axial):
            at = c * axial + z
            trace_s[at : at + 1, :] = edge_s[c, z, 7:8, :]
    trace_hi, trace_lo = split(trace_s[...])
    for q in range(per_row):
        block_hi[2 * axial * q : 2 * axial * (q + 1), LANES * q : LANES * (q + 1)] = trace_hi
        block_lo[2 * axial * q : 2 * axial * (q + 1), LANES * q : LANES * (q + 1)] = trace_lo
    both = jnp.concatenate([table_hi, table_lo], axis=0)
    turned = (((1,), (1,)), ((), ()))
    first = lax.dot_general(both, block_hi[...], turned, preferred_element_type=F32)
    second = lax.dot_general(table_hi, block_lo[...], turned, preferred_element_type=F32)
    coefficients = first[:slot_rows] + (first[slot_rows:] + second)
    for o in range(count):
        send1[o] = coefficients[rows_each * o : rows_each * (o + 1)]
    recv1[pl.ds(me, 1)] = send1[pl.ds(me, 1)]

    pl.semaphore_wait(barrier, count - 1)

    def send_coefficients(its_region, its_slab):
        pltpu.make_async_remote_copy(
            src_ref=send1.at[its_region * slabs + its_slab],
            dst_ref=recv1.at[me],
            send_sem=a2a_send.at[0],
            recv_sem=a2a_recv.at[0],
            device_id=(its_region, its_slab),
            device_id_type=MESH,
        ).start()

    each_other(send_coefficients)

    load_b.wait()
    load_u.wait()

    def axial_copy(field, at, up):
        return pltpu.make_async_remote_copy(
            src_ref=field.at[:, pl.ds(axial if up else 1, 1), cells, :],
            dst_ref=field.at[:, pl.ds(0 if up else axial + 1, 1), cells, :],
            send_sem=ax_send.at[at],
            recv_sem=ax_recv.at[at],
            device_id=(region, slab + 1 if up else slab - 1),
            device_id_type=MESH,
        )

    up_copies = [axial_copy(b_s, 0, True), axial_copy(u_s, 1, True)]
    down_copies = [axial_copy(b_s, 2, False), axial_copy(u_s, 3, False)]

    @pl.when(slab < slabs - 1)
    def _():
        for copy in up_copies:
            copy.start()

    @pl.when(slab > 0)
    def _():
        for copy in down_copies:
            copy.start()

    lane = iota((radial, LANES), 1)
    pair = lax.rem(lane + 1, LANES) // 2

    def pack(z, totals):
        totals = list(totals)
        for f, field in enumerate((b_s, u_s)):
            for c in range(3):
                at = c * axial + z
                plane = field[c, z + 1, PAD : PAD + radial, :]
                totals[f] = jnp.where(pair == at, pltpu.roll(plane, 2 * at, 1), totals[f])
                field[c, z + 1, PAD - 1 : PAD, :] = plane[0:1]
                field[c, z + 1, PAD + radial : PAD + radial + 1, :] = plane[radial - 1 : radial]
        return tuple(totals)

    nothing = jnp.zeros((radial, LANES), F32)
    pack_s[0], pack_s[1] = lax.fori_loop(0, axial, pack, (nothing, nothing), unroll=2)

    left = lax.rem(region + regions - 1, regions)
    right = lax.rem(region + 1, regions)

    def azimuth_copy(at, target):
        return pltpu.make_async_remote_copy(
            src_ref=pack_s,
            dst_ref=around_s.at[at],
            send_sem=az_send.at[at],
            recv_sem=az_recv.at[at],
            device_id=(target, slab),
            device_id_type=MESH,
        )

    azimuth_copies = [azimuth_copy(0, right)]
    if regions > 2:
        azimuth_copies.append(azimuth_copy(1, left))
    for copy in azimuth_copies:
        copy.start()

    single = (mode == 0.0) | (mode == azimuth_total - 1.0)
    weight_hi[...], weight_lo[...] = split(table * (jnp.where(single, 1.0, 2.0) / azimuth_total))

    shape = (radial, LANES)
    radius = 1.0 - (radial - iota(shape, 0).astype(F32) - 0.5) * RADIAL_STEP
    inverse = 1.0 / radius
    angle_step = 2.0 * math.pi / azimuth_total
    kr = TIME_STEP * DIFFUSIVITY / RADIAL_STEP**2
    kz = TIME_STEP * DIFFUSIVITY / AXIAL_STEP**2
    ar = TIME_STEP / (2.0 * RADIAL_STEP)
    az = TIME_STEP / (2.0 * AXIAL_STEP)
    kp = inverse * inverse * (TIME_STEP * DIFFUSIVITY / angle_step**2)
    radial_s[0] = inverse * (TIME_STEP / (2.0 * angle_step))
    radial_s[1] = kp
    radial_s[2] = inverse * (TIME_STEP * DIFFUSIVITY / (2.0 * RADIAL_STEP))
    radial_s[3] = (1.0 - 2.0 * kr - 2.0 * kz) - 2.0 * kp

    @pl.when(slab == 0)
    def _():
        for field in (b_s, u_s):
            field[:, 0, PAD : PAD + radial, :] = jnp.zeros((3, radial, LANES), F32)

    @pl.when(slab == slabs - 1)
    def _():
        for field in (b_s, u_s):
            field[:, axial + 1, PAD : PAD + radial, :] = jnp.zeros((3, radial, LANES), F32)

    load_w.wait()
    for s in range(mode_count):
        whi_s[s], wlo_s[s] = split(wall_s[s])

    def wait_all(buffer, sem):
        part = buffer.at[pl.ds(0, count - 1)]
        pltpu.make_async_copy(part, part, sem).wait()

    wait_all(recv1, a2a_recv.at[0])
    shape = (axial, LANES)
    own_cell = lax.rem(iota(shape, 1), axial) == iota(shape, 0)
    for j in range(slabs):
        got = recv1[j]
        for g in range(1, regions):
            got = got + recv1[g * slabs + j]
        for r in range(rows_each):
            hi, lo = split(jnp.where(own_cell, got[r : r + 1], 0.0))
            spread_s[r, 0, axial * j : axial * (j + 1), :] = hi
            spread_s[r, 1, axial * j : axial * (j + 1), :] = lo
    shape = (LANES, LANES)
    group = jnp.where(iota(shape, 0) // axial == iota(shape, 1) // axial, 1.0, 0.0).astype(BF16)
    shape = (nz, LANES)
    own_lane = lax.rem(iota(shape, 1), axial) == lax.rem(iota(shape, 0), axial)
    lane_group = iota(shape, 1) // (2 * axial)
    for r in range(rows_each):
        hi = jnp.dot(spread_s[r, 0], group, preferred_element_type=F32).astype(BF16)
        lo = jnp.dot(spread_s[r, 1], group, preferred_element_type=F32).astype(BF16)
        both = jnp.concatenate([hi, lo], axis=1)
        total = jnp.zeros((nz, LANES), F32)
        for q in range(per_row):
            s = r * per_row + q
            first = jnp.dot(whi_s[s], both, preferred_element_type=F32)
            second = jnp.dot(wlo_s[s], hi, preferred_element_type=F32)
            answer = first[:, :LANES] + (first[:, LANES:] + second)
            total = jnp.where(own_lane & (lane_group == q), answer, total)
        message = jnp.sum(total.reshape(slabs, axial, LANES), axis=1)
        for j in range(slabs):
            send2[j, r : r + 1, :] = message[j : j + 1]
    recv2[pl.ds(me, 1)] = send2[pl.ds(slab, 1)]

    def send_responses(its_region, its_slab):
        pltpu.make_async_remote_copy(
            src_ref=send2.at[its_slab],
            dst_ref=recv2.at[me],
            send_sem=a2a_send.at[1],
            recv_sem=a2a_recv.at[1],
            device_id=(its_region, its_slab),
            device_id_type=MESH,
        ).start()

    each_other(send_responses)

    for copy in azimuth_copies:
        copy.wait()

    even = lax.rem(lane, 2) == 0
    for f in range(2):
        from_left = around_s[0, f]
        from_right = around_s[len(azimuth_copies) - 1, f]
        halo_s[f] = jnp.where(
            even, pltpu.roll(from_left, 1, 1), pltpu.roll(from_right, LANES - 1, 1)
        )

    @pl.when(slab < slabs - 1)
    def _():
        for copy in up_copies:
            copy.wait_send()
        for copy in down_copies:
            copy.wait_recv()

    @pl.when(slab > 0)
    def _():
        for copy in down_copies:
            copy.wait_send()
        for copy in up_copies:
            copy.wait_recv()

    depth = 16
    first_lane = iota((depth, LANES), 1) == 0
    last_lane = iota((depth, LANES), 1) == LANES - 1

    def advance(z, carry):
        for start in range(0, radial, depth):
            rows = slice(PAD + start, PAD + start + depth)
            above = slice(PAD + start + 1, PAD + start + depth + 1)
            below = slice(PAD + start - 1, PAD + start + depth - 1)
            here = slice(start, start + depth)
            ap = radial_s[0, here, :]
            kp = radial_s[1, here, :]
            k1 = radial_s[2, here, :]
            kc = radial_s[3, here, :]

            def around(f, c, center):
                shift = lax.rem(LANES - lax.rem(2 * (c * axial + z), LANES), LANES)
                halo = pltpu.roll(halo_s[f, here, :], shift, 1)
                before = jnp.where(first_lane, halo, pltpu.roll(center, 1, 1))
                after = jnp.where(last_lane, halo, pltpu.roll(center, LANES - 1, 1))
                return before, after

            b = [b_s[c, z + 1, rows, :] for c in range(3)]
            u = [u_s[c, z + 1, rows, :] for c in range(3)]
            ur, up, uz = ar * u[0] - k1, ap * u[1], az * u[2]
            br, bp, bz = ar * b[0], ap * b[1], az * b[2]
            r_next, r_last = kr - ur, kr + ur
            p_next, p_last = kp - up, kp + up
            z_next, z_last = kz - uz, kz + uz
            for c in range(3):
                before, after = around(0, c, b[c])
                value = b[c] * kc
                value += r_next * b_s[c, z + 1, above, :] + r_last * b_s[c, z + 1, below, :]
                value += p_next * after + p_last * before
                value += z_next * b_s[c, z + 2, rows, :] + z_last * b_s[c, z, rows, :]
                before, after = around(1, c, u[c])
                value += br * (u_s[c, z + 1, above, :] - u_s[c, z + 1, below, :])
                value += bp * (after - before)
                value += bz * (u_s[c, z + 2, rows, :] - u_s[c, z, rows, :])
                out_s[c, z, here, :] = value
        return carry

    lax.fori_loop(0, axial, advance, 0, unroll=2)
    load_layers.wait()
    for z in range(axial):
        trace_s[z : z + 1, :] = u_s[0, z + 1, PAD + radial - 1 : PAD + radial, :]
    outer = kr + radial_s[2, radial - 1 : radial, :] - ar * trace_s[0:axial, :]
    outer_s[...] = outer * (layer_s[...].astype(F32) * (1.0 / LW))
    wait_all(recv2, a2a_recv.at[1])
    for o in range(count):
        row_s[rows_each * o : rows_each * (o + 1), :] = recv2[o]
    wait_all(recv1, a2a_send.at[0])
    wait_all(recv2, a2a_send.at[1])


def finish_kernel(
    out_ref, row_ref, weight_hi, weight_lo, outer_ref, next_hbm, flux_hbm, edge_s, flux_s, sem
):
    _, axial, radial, _ = out_ref.shape
    top = radial - 8
    inner = pltpu.make_async_copy(
        out_ref.at[:, :, 0:top, :], next_hbm.at[:, :, 0:top, :], sem.at[0]
    )
    inner.start()
    hi, lo = split(row_ref[...].T)
    flux = jnp.zeros((2 * axial, LANES), F32)
    for q in range(LANES // (2 * axial)):
        part = slice(2 * axial * q, 2 * axial * (q + 1))
        lanes = slice(LANES * q, LANES * (q + 1))
        flux += jnp.dot(hi[part], weight_hi[:, lanes], preferred_element_type=F32)
        flux += jnp.dot(lo[part], weight_hi[:, lanes], preferred_element_type=F32)
        flux += jnp.dot(hi[part], weight_lo[:, lanes], preferred_element_type=F32)
    flux_s[...] = flux
    store_flux = pltpu.make_async_copy(flux_s, flux_hbm, sem.at[1])
    store_flux.start()
    outer = outer_ref[...]
    last = iota((8, LANES), 0) == 7
    for z in range(axial):
        edge_s[0, z] = out_ref[0, z, top:radial, :]
    for c in range(2):
        change = flux[axial * c : axial * (c + 1)] * outer
        for z in range(axial):
            edge = out_ref[c + 1, z, top:radial, :]
            edge_s[c + 1, z] = jnp.where(last, edge - change[z : z + 1], edge)
    store_edge = pltpu.make_async_copy(edge_s, next_hbm.at[:, :, top:radial, :], sem.at[2])
    store_edge.start()
    inner.wait()
    store_flux.wait()
    store_edge.wait()


def solution(mesh):
    regions = mesh.shape["region"]
    slabs = mesh.shape["slab"]
    count = regions * slabs

    def shards(magnetic, velocity, wall_response, mode_slots, wall_layers):
        _, axial, radial, azimuth = magnetic.shape
        azimuth_total = mode_slots.shape[0]
        mode_count, nz, _ = wall_response.shape
        rows_each = mode_count * 2 * axial // LANES
        per_row = LANES // (2 * axial)
        slot_rows = count * rows_each
        vmem = pl.BlockSpec(memory_space=pltpu.VMEM)
        hbm = pl.BlockSpec(memory_space=pltpu.HBM)
        field = pltpu.VMEM((3, axial + 2, radial + 2 * PAD, azimuth), F32)
        kept = pl.pallas_call(
            functools.partial(step_kernel, regions, slabs),
            out_shape=(
                pltpu.VMEM(magnetic.shape, F32),
                pltpu.VMEM((slot_rows, LANES), F32),
                pltpu.VMEM((slot_rows, per_row * LANES), BF16),
                pltpu.VMEM((slot_rows, per_row * LANES), BF16),
                pltpu.VMEM((axial, LANES), F32),
            ),
            in_specs=[hbm] * 5,
            out_specs=(vmem,) * 5,
            scratch_shapes=[
                field,
                field,
                pltpu.VMEM((1, azimuth_total), jnp.int32),
                pltpu.VMEM((1, azimuth), jnp.int32),
                pltpu.VMEM(wall_response.shape, F32),
                pltpu.VMEM(wall_response.shape, BF16),
                pltpu.VMEM(wall_response.shape, BF16),
                pltpu.VMEM((2, axial, 8, LANES), F32),
                pltpu.VMEM((2 * axial, LANES), F32),
                pltpu.VMEM((LANES, per_row * LANES), BF16),
                pltpu.VMEM((LANES, per_row * LANES), BF16),
                pltpu.VMEM((4, radial, LANES), F32),
                pltpu.VMEM((rows_each, 2, nz, LANES), BF16),
                pltpu.VMEM((count, rows_each, LANES), F32),
                pltpu.VMEM((count, rows_each, LANES), F32),
                pltpu.VMEM((slabs, rows_each, LANES), F32),
                pltpu.VMEM((count, rows_each, LANES), F32),
                pltpu.VMEM((2, radial, LANES), F32),
                pltpu.VMEM((2, 2, radial, LANES), F32),
                pltpu.VMEM((2, radial, LANES), F32),
                pltpu.SemaphoreType.DMA((6,)),
                pltpu.SemaphoreType.DMA((2,)),
                pltpu.SemaphoreType.DMA((2,)),
                pltpu.SemaphoreType.DMA((4,)),
                pltpu.SemaphoreType.DMA((4,)),
                pltpu.SemaphoreType.DMA((2,)),
                pltpu.SemaphoreType.DMA((2,)),
            ],
            compiler_params=pltpu.CompilerParams(
                collective_id=0, has_side_effects=True, vmem_limit_bytes=48 * 1024 * 1024
            ),
            name="wall_step",
        )(
            *(
                pltpu.with_memory_space_constraint(x, pltpu.HBM)
                for x in (
                    mode_slots.reshape(1, azimuth_total),
                    wall_layers.reshape(1, azimuth),
                    magnetic,
                    velocity,
                    wall_response,
                )
            )
        )
        magnetic_next, flux = pl.pallas_call(
            finish_kernel,
            out_shape=(
                jax.ShapeDtypeStruct(magnetic.shape, F32),
                jax.ShapeDtypeStruct((2 * axial, azimuth), F32),
            ),
            in_specs=[vmem] * 5,
            out_specs=(hbm, hbm),
            scratch_shapes=[
                pltpu.VMEM((3, axial, 8, LANES), F32),
                pltpu.VMEM((2 * axial, LANES), F32),
                pltpu.SemaphoreType.DMA((3,)),
            ],
            compiler_params=pltpu.CompilerParams(vmem_limit_bytes=48 * 1024 * 1024),
            name="wall_finish",
        )(*(pltpu.with_memory_space_constraint(x, pltpu.VMEM) for x in kept))
        return magnetic_next, flux.reshape(2, axial, azimuth)

    placed = (
        P(None, "slab", None, "region"),
        P(None, "slab", None, "region"),
        P(("region", "slab"), None, None),
        P(),
        P("region"),
    )
    return jax.shard_map(
        shards,
        mesh=mesh,
        in_specs=placed,
        out_specs=(P(None, "slab", None, "region"), P(None, "slab", "region")),
        check_vma=False,
    )
```

```python
import functools
import math

import jax
import jax.numpy as jnp
from jax import lax
from jax.experimental import pallas as pl
from jax.experimental.pallas import tpu as pltpu
from jax.sharding import PartitionSpec as P

LW = 8
TIME_STEP = 0.0003
DIFFUSIVITY = 0.001
RADIAL_STEP = 1.0 / 384.0
AXIAL_STEP = 1.0 / 768.0
MESH = pl.DeviceIdType.MESH
F32 = jnp.float32
BF16 = jnp.bfloat16

PAD = 8
LANES = 128


def iota(shape, dim):
    return lax.broadcasted_iota(jnp.int32, shape, dim)


def split(x):
    hi = x.astype(BF16)
    return hi, (x - hi.astype(F32)).astype(BF16)


def sine(t):
    s = t * t
    value = 1.0 / math.factorial(13)
    for n in (11, 9, 7, 5, 3, 1):
        sign = 1.0 if (n // 2) % 2 == 0 else -1.0
        value = value * s + sign / math.factorial(n)
    return value * t


def step_kernel(
    regions,
    slabs,
    mode_ref,
    layer_ref,
    mag_hbm,
    vel_hbm,
    wall_hbm,
    out_s,
    row_s,
    weight_hi,
    weight_lo,
    outer_s,
    b_s,
    u_s,
    mode_s,
    layer_s,
    wall_s,
    whi_s,
    wlo_s,
    edge_s,
    trace_s,
    block_hi,
    block_lo,
    radial_s,
    spread_s,
    send1,
    recv1,
    send2,
    recv2,
    pack_s,
    around_s,
    halo_s,
    load_sem,
    a2a_send,
    a2a_recv,
    ax_send,
    ax_recv,
    az_send,
    az_recv,
):
    count = regions * slabs
    radial = mag_hbm.shape[2]
    axial = mag_hbm.shape[1]
    azimuth_total = mode_s.shape[1]
    mode_count, nz, _ = wall_hbm.shape
    rows_each = send1.shape[1]
    slot_rows = count * rows_each
    per_row = LANES // (2 * axial)
    region = lax.axis_index("region")
    slab = lax.axis_index("slab")
    me = region * slabs + slab
    cells = pl.ds(PAD, radial)

    load_b = pltpu.make_async_copy(mag_hbm, b_s.at[:, 1 : axial + 1, cells, :], load_sem.at[0])
    load_u = pltpu.make_async_copy(vel_hbm, u_s.at[:, 1 : axial + 1, cells, :], load_sem.at[1])
    load_w = pltpu.make_async_copy(wall_hbm, wall_s, load_sem.at[2])
    load_modes = pltpu.make_async_copy(mode_ref, mode_s, load_sem.at[3])
    load_layers = pltpu.make_async_copy(layer_ref, layer_s, load_sem.at[4])
    load_trace = pltpu.make_async_copy(
        mag_hbm.at[1:3, :, radial - 8 : radial, :], edge_s, load_sem.at[5]
    )
    load_modes.start()
    load_trace.start()
    load_b.start()
    load_u.start()
    load_layers.start()
    load_w.start()

    barrier = pltpu.get_barrier_semaphore()

    def each_other(act):
        for step in range(regions):
            its_region = lax.rem(region + step, regions)

            @pl.loop(0 if step else 1, slabs)
            def _(i, its_region=its_region):
                act(its_region, lax.rem(slab + i, slabs))

    def greet(its_region, its_slab):
        pl.semaphore_signal(
            barrier, inc=1, device_id=(its_region, its_slab), device_id_type=MESH
        )

    each_other(greet)

    shape = (radial, LANES)
    radius = 1.0 - (radial - iota(shape, 0).astype(F32) - 0.5) * RADIAL_STEP
    inverse = 1.0 / radius
    angle_step = 2.0 * math.pi / azimuth_total
    kr = TIME_STEP * DIFFUSIVITY / RADIAL_STEP**2
    kz = TIME_STEP * DIFFUSIVITY / AXIAL_STEP**2
    ar = TIME_STEP / (2.0 * RADIAL_STEP)
    az = TIME_STEP / (2.0 * AXIAL_STEP)
    kp = inverse * inverse * (TIME_STEP * DIFFUSIVITY / angle_step**2)
    radial_s[0] = inverse * (TIME_STEP / (2.0 * angle_step))
    radial_s[1] = kp
    radial_s[2] = inverse * (TIME_STEP * DIFFUSIVITY / (2.0 * RADIAL_STEP))
    radial_s[3] = (1.0 - 2.0 * kr - 2.0 * kz) - 2.0 * kp

    block_hi[...] = jnp.zeros(block_hi.shape, BF16)
    block_lo[...] = jnp.zeros(block_lo.shape, BF16)
    shape = (azimuth_total, per_row * LANES)
    picks = jnp.where(lax.rem(iota(shape, 0), per_row) == iota(shape, 1) // LANES, 1.0, 0.0)
    shape = (slot_rows, azimuth_total)
    mine = iota(shape, 1) // per_row == iota(shape, 0)
    load_modes.wait()
    modes = mode_s[...].astype(F32)
    tens = jnp.floor(modes * (1.0 / 32.0))
    parts = [jnp.where(mine, part, 0.0) for part in (tens, modes - 32.0 * tens)]
    parts = jnp.dot(
        jnp.concatenate(parts, axis=0).astype(BF16),
        picks.astype(BF16),
        preferred_element_type=F32,
    )
    mode = 32.0 * parts[:slot_rows] + parts[slot_rows:]
    half = jnp.floor(mode * 0.5)
    odd = mode - 2.0 * half
    cell = region * LANES + lax.rem(iota(mode.shape, 1), LANES)
    turn = (half + odd) * (2 * cell + 1).astype(F32) - odd * (azimuth_total // 2)
    turn = turn * (0.5 / azimuth_total)
    turn = turn - jnp.floor(turn + 0.5)
    table = sine((0.25 - jnp.abs(turn)) * (2.0 * math.pi))
    table_hi, table_lo = split(table)

    load_trace.wait()
    for c in range(2):
        for z in range(axial):
            at = c * axial + z
            trace_s[at : at + 1, :] = edge_s[c, z, 7:8, :]
    trace_hi, trace_lo = split(trace_s[...])
    for q in range(per_row):
        block_hi[2 * axial * q : 2 * axial * (q + 1), LANES * q : LANES * (q + 1)] = trace_hi
        block_lo[2 * axial * q : 2 * axial * (q + 1), LANES * q : LANES * (q + 1)] = trace_lo
    both = jnp.concatenate([table_hi, table_lo], axis=0)
    turned = (((1,), (1,)), ((), ()))
    first = lax.dot_general(both, block_hi[...], turned, preferred_element_type=F32)
    second = lax.dot_general(table_hi, block_lo[...], turned, preferred_element_type=F32)
    coefficients = first[:slot_rows] + (first[slot_rows:] + second)
    for o in range(count):
        send1[o] = coefficients[rows_each * o : rows_each * (o + 1)]
    recv1[pl.ds(me, 1)] = send1[pl.ds(me, 1)]

    pl.semaphore_wait(barrier, count - 1)

    def send_coefficients(its_region, its_slab):
        pltpu.make_async_remote_copy(
            src_ref=send1.at[its_region * slabs + its_slab],
            dst_ref=recv1.at[me],
            send_sem=a2a_send.at[0],
            recv_sem=a2a_recv.at[0],
            device_id=(its_region, its_slab),
            device_id_type=MESH,
        ).start()

    each_other(send_coefficients)

    load_b.wait()
    load_u.wait()

    def axial_copy(field, at, up):
        return pltpu.make_async_remote_copy(
            src_ref=field.at[:, pl.ds(axial if up else 1, 1), cells, :],
            dst_ref=field.at[:, pl.ds(0 if up else axial + 1, 1), cells, :],
            send_sem=ax_send.at[at],
            recv_sem=ax_recv.at[at],
            device_id=(region, slab + 1 if up else slab - 1),
            device_id_type=MESH,
        )

    up_copies = [axial_copy(b_s, 0, True), axial_copy(u_s, 1, True)]
    down_copies = [axial_copy(b_s, 2, False), axial_copy(u_s, 3, False)]

    @pl.when(slab < slabs - 1)
    def _():
        for copy in up_copies:
            copy.start()

    @pl.when(slab > 0)
    def _():
        for copy in down_copies:
            copy.start()

    lane = iota((radial, LANES), 1)
    pair = lax.rem(lane + 1, LANES) // 2

    def pack(z, totals):
        totals = list(totals)
        for f, field in enumerate((b_s, u_s)):
            for c in range(3):
                at = c * axial + z
                plane = field[c, z + 1, PAD : PAD + radial, :]
                totals[f] = jnp.where(pair == at, pltpu.roll(plane, 2 * at, 1), totals[f])
                field[c, z + 1, PAD - 1 : PAD, :] = plane[0:1]
                field[c, z + 1, PAD + radial : PAD + radial + 1, :] = plane[radial - 1 : radial]
        return tuple(totals)

    nothing = jnp.zeros((radial, LANES), F32)
    pack_s[0], pack_s[1] = lax.fori_loop(0, axial, pack, (nothing, nothing), unroll=2)

    left = lax.rem(region + regions - 1, regions)
    right = lax.rem(region + 1, regions)

    def azimuth_copy(at, target):
        return pltpu.make_async_remote_copy(
            src_ref=pack_s,
            dst_ref=around_s.at[at],
            send_sem=az_send.at[at],
            recv_sem=az_recv.at[at],
            device_id=(target, slab),
            device_id_type=MESH,
        )

    azimuth_copies = [azimuth_copy(0, right)]
    if regions > 2:
        azimuth_copies.append(azimuth_copy(1, left))
    for copy in azimuth_copies:
        copy.start()

    single = (mode == 0.0) | (mode == azimuth_total - 1.0)
    weight_hi[...], weight_lo[...] = split(table * (jnp.where(single, 1.0, 2.0) / azimuth_total))

    @pl.when(slab == 0)
    def _():
        for field in (b_s, u_s):
            field[:, 0, PAD : PAD + radial, :] = jnp.zeros((3, radial, LANES), F32)

    @pl.when(slab == slabs - 1)
    def _():
        for field in (b_s, u_s):
            field[:, axial + 1, PAD : PAD + radial, :] = jnp.zeros((3, radial, LANES), F32)

    load_w.wait()

    @pl.loop(0, mode_count)
    def _(s):
        hi, lo = split(wall_s[s])
        at = pl.ds(pl.multiple_of(s * nz, nz), nz)
        whi_s[at, :] = hi
        wlo_s[at, :] = lo


    def wait_all(buffer, sem):
        part = buffer.at[pl.ds(0, count - 1)]
        pltpu.make_async_copy(part, part, sem).wait()

    wait_all(recv1, a2a_recv.at[0])
    shape = (axial, LANES)
    own_cell = lax.rem(iota(shape, 1), axial) == iota(shape, 0)
    for j in range(slabs):
        got = recv1[j]
        for g in range(1, regions):
            got = got + recv1[g * slabs + j]
        for r in range(rows_each):
            hi, lo = split(jnp.where(own_cell, got[r : r + 1], 0.0))
            at = 2 * nz * r + axial * j
            spread_s[at : at + axial, :] = hi
            spread_s[at + nz : at + nz + axial, :] = lo
    shape = (LANES, LANES)
    group = jnp.where(iota(shape, 0) // axial == iota(shape, 1) // axial, 1.0, 0.0).astype(BF16)
    shape = (nz, LANES)
    own_lane = lax.rem(iota(shape, 1), axial) == lax.rem(iota(shape, 0), axial)
    lane_group = iota(shape, 1) // (2 * axial)
    repeated = jnp.dot(spread_s[...], group, preferred_element_type=F32).astype(BF16)
    for r in range(rows_each):
        hi = repeated[2 * nz * r : 2 * nz * r + nz]
        lo = repeated[2 * nz * r + nz : 2 * nz * (r + 1)]
        both = jnp.concatenate([hi, lo], axis=1)
        slots = slice(nz * per_row * r, nz * per_row * (r + 1))
        first = jnp.dot(whi_s[slots, :], both, preferred_element_type=F32)
        second = jnp.dot(wlo_s[slots, :], hi, preferred_element_type=F32)
        answer = first[:, :LANES] + (first[:, LANES:] + second)
        total = jnp.zeros((nz, LANES), F32)
        for q in range(per_row):
            part = answer[nz * q : nz * (q + 1)]
            total = jnp.where(own_lane & (lane_group == q), part, total)
        message = jnp.sum(total.reshape(slabs, axial, LANES), axis=1)
        for j in range(slabs):
            send2[j, r : r + 1, :] = message[j : j + 1]
    recv2[pl.ds(me, 1)] = send2[pl.ds(slab, 1)]

    def send_responses(its_region, its_slab):
        pltpu.make_async_remote_copy(
            src_ref=send2.at[its_slab],
            dst_ref=recv2.at[me],
            send_sem=a2a_send.at[1],
            recv_sem=a2a_recv.at[1],
            device_id=(its_region, its_slab),
            device_id_type=MESH,
        ).start()

    each_other(send_responses)

    for copy in azimuth_copies:
        copy.wait()

    even = lax.rem(lane, 2) == 0
    for f in range(2):
        from_left = around_s[0, f]
        from_right = around_s[len(azimuth_copies) - 1, f]
        halo_s[f] = jnp.where(
            even, pltpu.roll(from_left, 1, 1), pltpu.roll(from_right, LANES - 1, 1)
        )

    @pl.when(slab < slabs - 1)
    def _():
        for copy in up_copies:
            copy.wait_send()
        for copy in down_copies:
            copy.wait_recv()

    @pl.when(slab > 0)
    def _():
        for copy in down_copies:
            copy.wait_send()
        for copy in up_copies:
            copy.wait_recv()

    depth = 16
    first_lane = iota((depth, LANES), 1) == 0
    last_lane = iota((depth, LANES), 1) == LANES - 1

    def advance(z, carry):
        for start in range(0, radial, depth):
            rows = slice(PAD + start, PAD + start + depth)
            above = slice(PAD + start + 1, PAD + start + depth + 1)
            below = slice(PAD + start - 1, PAD + start + depth - 1)
            here = slice(start, start + depth)
            ap = radial_s[0, here, :]
            kp = radial_s[1, here, :]
            k1 = radial_s[2, here, :]
            kc = radial_s[3, here, :]

            def around(f, c, center):
                shift = lax.rem(LANES - lax.rem(2 * (c * axial + z), LANES), LANES)
                halo = pltpu.roll(halo_s[f, here, :], shift, 1)
                before = jnp.where(first_lane, halo, pltpu.roll(center, 1, 1))
                after = jnp.where(last_lane, halo, pltpu.roll(center, LANES - 1, 1))
                return before, after

            b = [b_s[c, z + 1, rows, :] for c in range(3)]
            u = [u_s[c, z + 1, rows, :] for c in range(3)]
            ur, up, uz = ar * u[0] - k1, ap * u[1], az * u[2]
            br, bp, bz = ar * b[0], ap * b[1], az * b[2]
            r_next, r_last = kr - ur, kr + ur
            p_next, p_last = kp - up, kp + up
            z_next, z_last = kz - uz, kz + uz
            for c in range(3):
                before, after = around(0, c, b[c])
                value = b[c] * kc
                value += r_next * b_s[c, z + 1, above, :] + r_last * b_s[c, z + 1, below, :]
                value += p_next * after + p_last * before
                value += z_next * b_s[c, z + 2, rows, :] + z_last * b_s[c, z, rows, :]
                before, after = around(1, c, u[c])
                value += br * (u_s[c, z + 1, above, :] - u_s[c, z + 1, below, :])
                value += bp * (after - before)
                value += bz * (u_s[c, z + 2, rows, :] - u_s[c, z, rows, :])
                out_s[c, z, here, :] = value
        return carry

    lax.fori_loop(0, axial, advance, 0, unroll=2)
    load_layers.wait()
    for z in range(axial):
        trace_s[z : z + 1, :] = u_s[0, z + 1, PAD + radial - 1 : PAD + radial, :]
    outer = kr + radial_s[2, radial - 1 : radial, :] - ar * trace_s[0:axial, :]
    outer_s[...] = outer * (layer_s[...].astype(F32) * (1.0 / LW))
    wait_all(recv2, a2a_recv.at[1])
    for o in range(count):
        row_s[rows_each * o : rows_each * (o + 1), :] = recv2[o]
    wait_all(recv1, a2a_send.at[0])
    wait_all(recv2, a2a_send.at[1])


def finish_kernel(
    out_ref, row_ref, weight_hi, weight_lo, outer_ref, next_hbm, flux_hbm, edge_s, flux_s, sem
):
    _, axial, radial, _ = out_ref.shape
    top = radial - 8
    inner = pltpu.make_async_copy(
        out_ref.at[:, :, 0:top, :], next_hbm.at[:, :, 0:top, :], sem.at[0]
    )
    inner.start()
    hi, lo = split(row_ref[...].T)
    flux = jnp.zeros((2 * axial, LANES), F32)
    for q in range(LANES // (2 * axial)):
        part = slice(2 * axial * q, 2 * axial * (q + 1))
        lanes = slice(LANES * q, LANES * (q + 1))
        flux += jnp.dot(hi[part], weight_hi[:, lanes], preferred_element_type=F32)
        flux += jnp.dot(lo[part], weight_hi[:, lanes], preferred_element_type=F32)
        flux += jnp.dot(hi[part], weight_lo[:, lanes], preferred_element_type=F32)
    flux_s[...] = flux
    store_flux = pltpu.make_async_copy(flux_s, flux_hbm, sem.at[1])
    store_flux.start()
    outer = outer_ref[...]
    last = iota((8, LANES), 0) == 7
    for z in range(axial):
        edge_s[0, z] = out_ref[0, z, top:radial, :]
    for c in range(2):
        change = flux[axial * c : axial * (c + 1)] * outer
        for z in range(axial):
            edge = out_ref[c + 1, z, top:radial, :]
            edge_s[c + 1, z] = jnp.where(last, edge - change[z : z + 1], edge)
    store_edge = pltpu.make_async_copy(edge_s, next_hbm.at[:, :, top:radial, :], sem.at[2])
    store_edge.start()
    inner.wait()
    store_flux.wait()
    store_edge.wait()


def solution(mesh):
    regions = mesh.shape["region"]
    slabs = mesh.shape["slab"]
    count = regions * slabs

    def shards(magnetic, velocity, wall_response, mode_slots, wall_layers):
        _, axial, radial, azimuth = magnetic.shape
        azimuth_total = mode_slots.shape[0]
        mode_count, nz, _ = wall_response.shape
        rows_each = mode_count * 2 * axial // LANES
        per_row = LANES // (2 * axial)
        slot_rows = count * rows_each
        vmem = pl.BlockSpec(memory_space=pltpu.VMEM)
        hbm = pl.BlockSpec(memory_space=pltpu.HBM)
        field = pltpu.VMEM((3, axial + 2, radial + 2 * PAD, azimuth), F32)
        kept = pl.pallas_call(
            functools.partial(step_kernel, regions, slabs),
            out_shape=(
                pltpu.VMEM(magnetic.shape, F32),
                pltpu.VMEM((slot_rows, LANES), F32),
                pltpu.VMEM((slot_rows, per_row * LANES), BF16),
                pltpu.VMEM((slot_rows, per_row * LANES), BF16),
                pltpu.VMEM((axial, LANES), F32),
            ),
            in_specs=[hbm] * 5,
            out_specs=(vmem,) * 5,
            scratch_shapes=[
                field,
                field,
                pltpu.VMEM((1, azimuth_total), jnp.int32),
                pltpu.VMEM((1, azimuth), jnp.int32),
                pltpu.VMEM(wall_response.shape, F32),
                pltpu.VMEM((mode_count * nz, nz), BF16),
                pltpu.VMEM((mode_count * nz, nz), BF16),
                pltpu.VMEM((2, axial, 8, LANES), F32),
                pltpu.VMEM((2 * axial, LANES), F32),
                pltpu.VMEM((LANES, per_row * LANES), BF16),
                pltpu.VMEM((LANES, per_row * LANES), BF16),
                pltpu.VMEM((4, radial, LANES), F32),
                pltpu.VMEM((rows_each * 2 * nz, LANES), BF16),
                pltpu.VMEM((count, rows_each, LANES), F32),
                pltpu.VMEM((count, rows_each, LANES), F32),
                pltpu.VMEM((slabs, rows_each, LANES), F32),
                pltpu.VMEM((count, rows_each, LANES), F32),
                pltpu.VMEM((2, radial, LANES), F32),
                pltpu.VMEM((2, 2, radial, LANES), F32),
                pltpu.VMEM((2, radial, LANES), F32),
                pltpu.SemaphoreType.DMA((6,)),
                pltpu.SemaphoreType.DMA((2,)),
                pltpu.SemaphoreType.DMA((2,)),
                pltpu.SemaphoreType.DMA((4,)),
                pltpu.SemaphoreType.DMA((4,)),
                pltpu.SemaphoreType.DMA((2,)),
                pltpu.SemaphoreType.DMA((2,)),
            ],
            compiler_params=pltpu.CompilerParams(
                collective_id=0, has_side_effects=True, vmem_limit_bytes=48 * 1024 * 1024
            ),
            name="wall_step",
        )(
            *(
                pltpu.with_memory_space_constraint(x, pltpu.HBM)
                for x in (
                    mode_slots.reshape(1, azimuth_total),
                    wall_layers.reshape(1, azimuth),
                    magnetic,
                    velocity,
                    wall_response,
                )
            )
        )
        magnetic_next, flux = pl.pallas_call(
            finish_kernel,
            out_shape=(
                jax.ShapeDtypeStruct(magnetic.shape, F32),
                jax.ShapeDtypeStruct((2 * axial, azimuth), F32),
            ),
            in_specs=[vmem] * 5,
            out_specs=(hbm, hbm),
            scratch_shapes=[
                pltpu.VMEM((3, axial, 8, LANES), F32),
                pltpu.VMEM((2 * axial, LANES), F32),
                pltpu.SemaphoreType.DMA((3,)),
            ],
            compiler_params=pltpu.CompilerParams(vmem_limit_bytes=48 * 1024 * 1024),
            name="wall_finish",
        )(*(pltpu.with_memory_space_constraint(x, pltpu.VMEM) for x in kept))
        return magnetic_next, flux.reshape(2, axial, azimuth)

    placed = (
        P(None, "slab", None, "region"),
        P(None, "slab", None, "region"),
        P(("region", "slab"), None, None),
        P(),
        P("region"),
    )
    return jax.shard_map(
        shards,
        mesh=mesh,
        in_specs=placed,
        out_specs=(P(None, "slab", None, "region"), P(None, "slab", "region")),
        check_vma=False,
    )
```

```python
import functools
import math

import jax
import jax.numpy as jnp
from jax import lax
from jax.experimental import pallas as pl
from jax.experimental.pallas import tpu as pltpu
from jax.sharding import PartitionSpec as P

LW = 8
TIME_STEP = 0.0003
DIFFUSIVITY = 0.001
RADIAL_STEP = 1.0 / 384.0
AXIAL_STEP = 1.0 / 768.0
MESH = pl.DeviceIdType.MESH
F32 = jnp.float32
BF16 = jnp.bfloat16

PAD = 8
LANES = 128


def iota(shape, dim):
    return lax.broadcasted_iota(jnp.int32, shape, dim)


def high(x, n):
    if n & (n - 1):
        return x // n
    return lax.shift_right_logical(x, jnp.full(x.shape, n.bit_length() - 1, x.dtype))


def low(x, n):
    return lax.rem(x, n) if n & (n - 1) else x & (n - 1)


def split(x):
    hi = x.astype(BF16)
    return hi, (x - hi.astype(F32)).astype(BF16)


def sine(t):
    s = t * t
    value = 1.0 / math.factorial(13)
    for n in (11, 9, 7, 5, 3, 1):
        sign = 1.0 if (n // 2) % 2 == 0 else -1.0
        value = value * s + sign / math.factorial(n)
    return value * t


def step_kernel(
    regions,
    slabs,
    mode_ref,
    layer_ref,
    mag_hbm,
    vel_hbm,
    wall_hbm,
    out_s,
    row_s,
    weight_hi,
    weight_lo,
    outer_s,
    b_s,
    u_s,
    mode_s,
    layer_s,
    wall_s,
    whi_s,
    wlo_s,
    edge_s,
    trace_s,
    block_hi,
    block_lo,
    radial_s,
    spread_s,
    send1,
    recv1,
    send2,
    recv2,
    pack_s,
    around_s,
    halo_s,
    load_sem,
    a2a_send,
    a2a_recv,
    ax_send,
    ax_recv,
    az_send,
    az_recv,
):
    count = regions * slabs
    radial = mag_hbm.shape[2]
    axial = mag_hbm.shape[1]
    azimuth_total = mode_s.shape[1]
    mode_count, nz, _ = wall_hbm.shape
    rows_each = send1.shape[1]
    slot_rows = count * rows_each
    per_row = LANES // (2 * axial)
    region = lax.axis_index("region")
    slab = lax.axis_index("slab")
    me = region * slabs + slab
    cells = pl.ds(PAD, radial)

    load_b = pltpu.make_async_copy(mag_hbm, b_s.at[:, 1 : axial + 1, cells, :], load_sem.at[0])
    load_u = pltpu.make_async_copy(vel_hbm, u_s.at[:, 1 : axial + 1, cells, :], load_sem.at[1])
    load_w = pltpu.make_async_copy(wall_hbm, wall_s, load_sem.at[2])
    load_modes = pltpu.make_async_copy(mode_ref, mode_s, load_sem.at[3])
    load_layers = pltpu.make_async_copy(layer_ref, layer_s, load_sem.at[4])
    load_trace = pltpu.make_async_copy(
        mag_hbm.at[1:3, :, radial - 8 : radial, :], edge_s, load_sem.at[5]
    )
    load_modes.start()
    load_trace.start()
    load_b.start()
    load_u.start()
    load_layers.start()
    load_w.start()

    barrier = pltpu.get_barrier_semaphore()

    def each_other(act):
        for step in range(regions):
            its_region = lax.rem(region + step, regions)

            @pl.loop(0 if step else 1, slabs)
            def _(i, its_region=its_region):
                act(its_region, lax.rem(slab + i, slabs))

    def greet(its_region, its_slab):
        pl.semaphore_signal(
            barrier, inc=1, device_id=(its_region, its_slab), device_id_type=MESH
        )

    each_other(greet)

    shape = (radial, LANES)
    radius = 1.0 - (radial - iota(shape, 0).astype(F32) - 0.5) * RADIAL_STEP
    inverse = 1.0 / radius
    angle_step = 2.0 * math.pi / azimuth_total
    kr = TIME_STEP * DIFFUSIVITY / RADIAL_STEP**2
    kz = TIME_STEP * DIFFUSIVITY / AXIAL_STEP**2
    ar = TIME_STEP / (2.0 * RADIAL_STEP)
    az = TIME_STEP / (2.0 * AXIAL_STEP)
    kp = inverse * inverse * (TIME_STEP * DIFFUSIVITY / angle_step**2)
    radial_s[0] = inverse * (TIME_STEP / (2.0 * angle_step))
    radial_s[1] = kp
    radial_s[2] = inverse * (TIME_STEP * DIFFUSIVITY / (2.0 * RADIAL_STEP))
    radial_s[3] = (1.0 - 2.0 * kr - 2.0 * kz) - 2.0 * kp

    block_hi[...] = jnp.zeros(block_hi.shape, BF16)
    block_lo[...] = jnp.zeros(block_lo.shape, BF16)
    shape = (azimuth_total, per_row * LANES)
    picks = jnp.where(low(iota(shape, 0), per_row) == high(iota(shape, 1), LANES), 1.0, 0.0)
    shape = (slot_rows, azimuth_total)
    mine = high(iota(shape, 1), per_row) == iota(shape, 0)
    load_modes.wait()
    modes = mode_s[...].astype(F32)
    tens = jnp.floor(modes * (1.0 / 32.0))
    parts = [jnp.where(mine, part, 0.0) for part in (tens, modes - 32.0 * tens)]
    parts = jnp.dot(
        jnp.concatenate(parts, axis=0).astype(BF16),
        picks.astype(BF16),
        preferred_element_type=F32,
    )
    mode = 32.0 * parts[:slot_rows] + parts[slot_rows:]
    half = jnp.floor(mode * 0.5)
    odd = mode - 2.0 * half
    cell = region * LANES + low(iota(mode.shape, 1), LANES)
    turn = (half + odd) * (2 * cell + 1).astype(F32) - odd * (azimuth_total // 2)
    turn = turn * (0.5 / azimuth_total)
    turn = turn - jnp.floor(turn + 0.5)
    table = sine((0.25 - jnp.abs(turn)) * (2.0 * math.pi))
    table_hi, table_lo = split(table)

    load_trace.wait()
    for c in range(2):
        for z in range(axial):
            at = c * axial + z
            trace_s[at : at + 1, :] = edge_s[c, z, 7:8, :]
    trace_hi, trace_lo = split(trace_s[...])
    for q in range(per_row):
        block_hi[2 * axial * q : 2 * axial * (q + 1), LANES * q : LANES * (q + 1)] = trace_hi
        block_lo[2 * axial * q : 2 * axial * (q + 1), LANES * q : LANES * (q + 1)] = trace_lo
    both = jnp.concatenate([table_hi, table_lo], axis=0)
    turned = (((1,), (1,)), ((), ()))
    first = lax.dot_general(both, block_hi[...], turned, preferred_element_type=F32)
    second = lax.dot_general(table_hi, block_lo[...], turned, preferred_element_type=F32)
    coefficients = first[:slot_rows] + (first[slot_rows:] + second)
    for o in range(count):
        send1[o] = coefficients[rows_each * o : rows_each * (o + 1)]
    recv1[pl.ds(me, 1)] = send1[pl.ds(me, 1)]

    pl.semaphore_wait(barrier, count - 1)

    def send_coefficients(its_region, its_slab):
        pltpu.make_async_remote_copy(
            src_ref=send1.at[its_region * slabs + its_slab],
            dst_ref=recv1.at[me],
            send_sem=a2a_send.at[0],
            recv_sem=a2a_recv.at[0],
            device_id=(its_region, its_slab),
            device_id_type=MESH,
        ).start()

    each_other(send_coefficients)

    load_b.wait()
    load_u.wait()

    def axial_copy(field, at, up):
        return pltpu.make_async_remote_copy(
            src_ref=field.at[:, pl.ds(axial if up else 1, 1), cells, :],
            dst_ref=field.at[:, pl.ds(0 if up else axial + 1, 1), cells, :],
            send_sem=ax_send.at[at],
            recv_sem=ax_recv.at[at],
            device_id=(region, slab + 1 if up else slab - 1),
            device_id_type=MESH,
        )

    up_copies = [axial_copy(b_s, 0, True), axial_copy(u_s, 1, True)]
    down_copies = [axial_copy(b_s, 2, False), axial_copy(u_s, 3, False)]

    @pl.when(slab < slabs - 1)
    def _():
        for copy in up_copies:
            copy.start()

    @pl.when(slab > 0)
    def _():
        for copy in down_copies:
            copy.start()

    lane = iota((radial, LANES), 1)
    pair = high(low(lane + 1, LANES), 2)

    def pack(z, totals):
        totals = list(totals)
        for f, field in enumerate((b_s, u_s)):
            for c in range(3):
                at = c * axial + z
                plane = field[c, z + 1, PAD : PAD + radial, :]
                totals[f] = jnp.where(pair == at, pltpu.roll(plane, 2 * at, 1), totals[f])
                field[c, z + 1, PAD - 1 : PAD, :] = plane[0:1]
                field[c, z + 1, PAD + radial : PAD + radial + 1, :] = plane[radial - 1 : radial]
        return tuple(totals)

    nothing = jnp.zeros((radial, LANES), F32)
    pack_s[0], pack_s[1] = lax.fori_loop(0, axial, pack, (nothing, nothing), unroll=2)

    left = lax.rem(region + regions - 1, regions)
    right = lax.rem(region + 1, regions)

    def azimuth_copy(at, target):
        return pltpu.make_async_remote_copy(
            src_ref=pack_s,
            dst_ref=around_s.at[at],
            send_sem=az_send.at[at],
            recv_sem=az_recv.at[at],
            device_id=(target, slab),
            device_id_type=MESH,
        )

    azimuth_copies = [azimuth_copy(0, right)]
    if regions > 2:
        azimuth_copies.append(azimuth_copy(1, left))
    for copy in azimuth_copies:
        copy.start()

    single = (mode == 0.0) | (mode == azimuth_total - 1.0)
    weight_hi[...], weight_lo[...] = split(table * (jnp.where(single, 1.0, 2.0) / azimuth_total))

    @pl.when(slab == 0)
    def _():
        for field in (b_s, u_s):
            field[:, 0, PAD : PAD + radial, :] = jnp.zeros((3, radial, LANES), F32)

    @pl.when(slab == slabs - 1)
    def _():
        for field in (b_s, u_s):
            field[:, axial + 1, PAD : PAD + radial, :] = jnp.zeros((3, radial, LANES), F32)

    load_w.wait()

    @pl.loop(0, mode_count)
    def _(s):
        hi, lo = split(wall_s[s])
        at = pl.ds(pl.multiple_of(s * nz, nz), nz)
        whi_s[at, :] = hi
        wlo_s[at, :] = lo


    def wait_all(buffer, sem):
        part = buffer.at[pl.ds(0, count - 1)]
        pltpu.make_async_copy(part, part, sem).wait()

    wait_all(recv1, a2a_recv.at[0])
    shape = (axial, LANES)
    own_cell = low(iota(shape, 1), axial) == iota(shape, 0)
    for j in range(slabs):
        got = recv1[j]
        for g in range(1, regions):
            got = got + recv1[g * slabs + j]
        for r in range(rows_each):
            hi, lo = split(jnp.where(own_cell, got[r : r + 1], 0.0))
            at = 2 * nz * r + axial * j
            spread_s[at : at + axial, :] = hi
            spread_s[at + nz : at + nz + axial, :] = lo
    shape = (LANES, LANES)
    group = jnp.where(high(iota(shape, 0), axial) == high(iota(shape, 1), axial), 1.0, 0.0).astype(BF16)
    shape = (nz, LANES)
    own_lane = low(iota(shape, 1), axial) == low(iota(shape, 0), axial)
    lane_group = high(iota(shape, 1), 2 * axial)
    repeated = jnp.dot(spread_s[...], group, preferred_element_type=F32).astype(BF16)
    for r in range(rows_each):
        hi = repeated[2 * nz * r : 2 * nz * r + nz]
        lo = repeated[2 * nz * r + nz : 2 * nz * (r + 1)]
        both = jnp.concatenate([hi, lo], axis=1)
        slots = slice(nz * per_row * r, nz * per_row * (r + 1))
        first = jnp.dot(whi_s[slots, :], both, preferred_element_type=F32)
        second = jnp.dot(wlo_s[slots, :], hi, preferred_element_type=F32)
        answer = first[:, :LANES] + (first[:, LANES:] + second)
        total = jnp.zeros((nz, LANES), F32)
        for q in range(per_row):
            part = answer[nz * q : nz * (q + 1)]
            total = jnp.where(own_lane & (lane_group == q), part, total)
        message = jnp.sum(total.reshape(slabs, axial, LANES), axis=1)
        for j in range(slabs):
            send2[j, r : r + 1, :] = message[j : j + 1]
    recv2[pl.ds(me, 1)] = send2[pl.ds(slab, 1)]

    def send_responses(its_region, its_slab):
        pltpu.make_async_remote_copy(
            src_ref=send2.at[its_slab],
            dst_ref=recv2.at[me],
            send_sem=a2a_send.at[1],
            recv_sem=a2a_recv.at[1],
            device_id=(its_region, its_slab),
            device_id_type=MESH,
        ).start()

    each_other(send_responses)

    for copy in azimuth_copies:
        copy.wait()

    even = low(lane, 2) == 0
    for f in range(2):
        from_left = around_s[0, f]
        from_right = around_s[len(azimuth_copies) - 1, f]
        halo_s[f] = jnp.where(
            even, pltpu.roll(from_left, 1, 1), pltpu.roll(from_right, LANES - 1, 1)
        )

    @pl.when(slab < slabs - 1)
    def _():
        for copy in up_copies:
            copy.wait_send()
        for copy in down_copies:
            copy.wait_recv()

    @pl.when(slab > 0)
    def _():
        for copy in down_copies:
            copy.wait_send()
        for copy in up_copies:
            copy.wait_recv()

    depth = 16
    first_row = PAD + slab // slabs
    first_lane = iota((depth, LANES), 1) == 0
    last_lane = iota((depth, LANES), 1) == LANES - 1

    def advance(z, carry):
        for start in range(0, radial, depth):
            rows = slice(PAD + start, PAD + start + depth)
            above = pl.ds(first_row + (start + 1), depth)
            below = pl.ds(first_row + (start - 1), depth)
            here = slice(start, start + depth)
            ap = radial_s[0, here, :]
            kp = radial_s[1, here, :]
            k1 = radial_s[2, here, :]
            kc = radial_s[3, here, :]

            def around(f, c, center):
                shift = low(LANES - 2 * (c * axial + z), LANES)
                halo = pltpu.roll(halo_s[f, here, :], shift, 1)
                before = jnp.where(first_lane, halo, pltpu.roll(center, 1, 1))
                after = jnp.where(last_lane, halo, pltpu.roll(center, LANES - 1, 1))
                return before, after

            b = [b_s[c, z + 1, rows, :] for c in range(3)]
            u = [u_s[c, z + 1, rows, :] for c in range(3)]
            ur, up, uz = ar * u[0] - k1, ap * u[1], az * u[2]
            br, bp, bz = ar * b[0], ap * b[1], az * b[2]
            r_next, r_last = kr - ur, kr + ur
            p_next, p_last = kp - up, kp + up
            z_next, z_last = kz - uz, kz + uz
            for c in range(3):
                before, after = around(0, c, b[c])
                value = b[c] * kc
                value += r_next * b_s[c, z + 1, above, :] + r_last * b_s[c, z + 1, below, :]
                value += p_next * after + p_last * before
                value += z_next * b_s[c, z + 2, rows, :] + z_last * b_s[c, z, rows, :]
                before, after = around(1, c, u[c])
                value += br * (u_s[c, z + 1, above, :] - u_s[c, z + 1, below, :])
                value += bp * (after - before)
                value += bz * (u_s[c, z + 2, rows, :] - u_s[c, z, rows, :])
                out_s[c, z, here, :] = value
        return carry

    lax.fori_loop(0, axial, advance, 0, unroll=2)
    load_layers.wait()
    for z in range(axial):
        trace_s[z : z + 1, :] = u_s[0, z + 1, PAD + radial - 1 : PAD + radial, :]
    outer = kr + radial_s[2, radial - 1 : radial, :] - ar * trace_s[0:axial, :]
    outer_s[...] = outer * (layer_s[...].astype(F32) * (1.0 / LW))
    wait_all(recv2, a2a_recv.at[1])
    for o in range(count):
        row_s[rows_each * o : rows_each * (o + 1), :] = recv2[o]
    wait_all(recv1, a2a_send.at[0])
    wait_all(recv2, a2a_send.at[1])


def finish_kernel(
    out_ref, row_ref, weight_hi, weight_lo, outer_ref, next_hbm, flux_hbm, edge_s, flux_s, sem
):
    _, axial, radial, _ = out_ref.shape
    top = radial - 8
    inner = pltpu.make_async_copy(
        out_ref.at[:, :, 0:top, :], next_hbm.at[:, :, 0:top, :], sem.at[0]
    )
    inner.start()
    hi, lo = split(row_ref[...].T)
    flux = jnp.zeros((2 * axial, LANES), F32)
    for q in range(LANES // (2 * axial)):
        part = slice(2 * axial * q, 2 * axial * (q + 1))
        lanes = slice(LANES * q, LANES * (q + 1))
        flux += jnp.dot(hi[part], weight_hi[:, lanes], preferred_element_type=F32)
        flux += jnp.dot(lo[part], weight_hi[:, lanes], preferred_element_type=F32)
        flux += jnp.dot(hi[part], weight_lo[:, lanes], preferred_element_type=F32)
    flux_s[...] = flux
    store_flux = pltpu.make_async_copy(flux_s, flux_hbm, sem.at[1])
    store_flux.start()
    outer = outer_ref[...]
    last = iota((8, LANES), 0) == 7
    for z in range(axial):
        edge_s[0, z] = out_ref[0, z, top:radial, :]
    for c in range(2):
        change = flux[axial * c : axial * (c + 1)] * outer
        for z in range(axial):
            edge = out_ref[c + 1, z, top:radial, :]
            edge_s[c + 1, z] = jnp.where(last, edge - change[z : z + 1], edge)
    store_edge = pltpu.make_async_copy(edge_s, next_hbm.at[:, :, top:radial, :], sem.at[2])
    store_edge.start()
    inner.wait()
    store_flux.wait()
    store_edge.wait()


def solution(mesh):
    regions = mesh.shape["region"]
    slabs = mesh.shape["slab"]
    count = regions * slabs

    def shards(magnetic, velocity, wall_response, mode_slots, wall_layers):
        _, axial, radial, azimuth = magnetic.shape
        azimuth_total = mode_slots.shape[0]
        mode_count, nz, _ = wall_response.shape
        rows_each = mode_count * 2 * axial // LANES
        per_row = LANES // (2 * axial)
        slot_rows = count * rows_each
        vmem = pl.BlockSpec(memory_space=pltpu.VMEM)
        hbm = pl.BlockSpec(memory_space=pltpu.HBM)
        field = pltpu.VMEM((3, axial + 2, radial + 2 * PAD, azimuth), F32)
        kept = pl.pallas_call(
            functools.partial(step_kernel, regions, slabs),
            out_shape=(
                pltpu.VMEM(magnetic.shape, F32),
                pltpu.VMEM((slot_rows, LANES), F32),
                pltpu.VMEM((slot_rows, per_row * LANES), BF16),
                pltpu.VMEM((slot_rows, per_row * LANES), BF16),
                pltpu.VMEM((axial, LANES), F32),
            ),
            in_specs=[hbm] * 5,
            out_specs=(vmem,) * 5,
            scratch_shapes=[
                field,
                field,
                pltpu.VMEM((1, azimuth_total), jnp.int32),
                pltpu.VMEM((1, azimuth), jnp.int32),
                pltpu.VMEM(wall_response.shape, F32),
                pltpu.VMEM((mode_count * nz, nz), BF16),
                pltpu.VMEM((mode_count * nz, nz), BF16),
                pltpu.VMEM((2, axial, 8, LANES), F32),
                pltpu.VMEM((2 * axial, LANES), F32),
                pltpu.VMEM((LANES, per_row * LANES), BF16),
                pltpu.VMEM((LANES, per_row * LANES), BF16),
                pltpu.VMEM((4, radial, LANES), F32),
                pltpu.VMEM((rows_each * 2 * nz, LANES), BF16),
                pltpu.VMEM((count, rows_each, LANES), F32),
                pltpu.VMEM((count, rows_each, LANES), F32),
                pltpu.VMEM((slabs, rows_each, LANES), F32),
                pltpu.VMEM((count, rows_each, LANES), F32),
                pltpu.VMEM((2, radial, LANES), F32),
                pltpu.VMEM((2, 2, radial, LANES), F32),
                pltpu.VMEM((2, radial, LANES), F32),
                pltpu.SemaphoreType.DMA((6,)),
                pltpu.SemaphoreType.DMA((2,)),
                pltpu.SemaphoreType.DMA((2,)),
                pltpu.SemaphoreType.DMA((4,)),
                pltpu.SemaphoreType.DMA((4,)),
                pltpu.SemaphoreType.DMA((2,)),
                pltpu.SemaphoreType.DMA((2,)),
            ],
            compiler_params=pltpu.CompilerParams(
                collective_id=0, has_side_effects=True, vmem_limit_bytes=48 * 1024 * 1024
            ),
            name="wall_step",
        )(
            *(
                pltpu.with_memory_space_constraint(x, pltpu.HBM)
                for x in (
                    mode_slots.reshape(1, azimuth_total),
                    wall_layers.reshape(1, azimuth),
                    magnetic,
                    velocity,
                    wall_response,
                )
            )
        )
        magnetic_next, flux = pl.pallas_call(
            finish_kernel,
            out_shape=(
                jax.ShapeDtypeStruct(magnetic.shape, F32),
                jax.ShapeDtypeStruct((2 * axial, azimuth), F32),
            ),
            in_specs=[vmem] * 5,
            out_specs=(hbm, hbm),
            scratch_shapes=[
                pltpu.VMEM((3, axial, 8, LANES), F32),
                pltpu.VMEM((2 * axial, LANES), F32),
                pltpu.SemaphoreType.DMA((3,)),
            ],
            compiler_params=pltpu.CompilerParams(vmem_limit_bytes=48 * 1024 * 1024),
            name="wall_finish",
        )(*(pltpu.with_memory_space_constraint(x, pltpu.VMEM) for x in kept))
        return magnetic_next, flux.reshape(2, axial, azimuth)

    placed = (
        P(None, "slab", None, "region"),
        P(None, "slab", None, "region"),
        P(("region", "slab"), None, None),
        P(),
        P("region"),
    )
    return jax.shard_map(
        shards,
        mesh=mesh,
        in_specs=placed,
        out_specs=(P(None, "slab", None, "region"), P(None, "slab", "region")),
        check_vma=False,
    )
```

```python
import functools
import math

import jax
import jax.numpy as jnp
from jax import lax
from jax.experimental import pallas as pl
from jax.experimental.pallas import tpu as pltpu
from jax.sharding import PartitionSpec as P

LW = 8
TIME_STEP = 0.0003
DIFFUSIVITY = 0.001
RADIAL_STEP = 1.0 / 384.0
AXIAL_STEP = 1.0 / 768.0
MESH = pl.DeviceIdType.MESH
F32 = jnp.float32
BF16 = jnp.bfloat16

PAD = 8
LANES = 128


def iota(shape, dim):
    return lax.broadcasted_iota(jnp.int32, shape, dim)


def high(x, n):
    if n & (n - 1):
        return x // n
    return lax.shift_right_logical(x, jnp.full(x.shape, n.bit_length() - 1, x.dtype))


def low(x, n):
    return lax.rem(x, n) if n & (n - 1) else x & (n - 1)


def split(x):
    hi = x.astype(BF16)
    return hi, (x - hi.astype(F32)).astype(BF16)


def sine(t):
    s = t * t
    value = 1.0 / math.factorial(13)
    for n in (11, 9, 7, 5, 3, 1):
        sign = 1.0 if (n // 2) % 2 == 0 else -1.0
        value = value * s + sign / math.factorial(n)
    return value * t


def step_kernel(
    regions,
    slabs,
    mode_ref,
    layer_ref,
    mag_hbm,
    vel_hbm,
    wall_hbm,
    out_s,
    row_s,
    weight_hi,
    weight_lo,
    outer_s,
    b_s,
    u_s,
    mode_s,
    layer_s,
    wall_s,
    whi_s,
    wlo_s,
    edge_s,
    trace_s,
    block_hi,
    block_lo,
    radial_s,
    spread_s,
    send1,
    recv1,
    send2,
    recv2,
    pack_s,
    around_s,
    halo_s,
    load_sem,
    a2a_send,
    a2a_recv,
    ax_send,
    ax_recv,
    az_send,
    az_recv,
):
    count = regions * slabs
    radial = mag_hbm.shape[2]
    axial = mag_hbm.shape[1]
    azimuth_total = mode_s.shape[1]
    mode_count, nz, _ = wall_hbm.shape
    rows_each = send1.shape[1]
    slot_rows = count * rows_each
    per_row = LANES // (2 * axial)
    region = lax.axis_index("region")
    slab = lax.axis_index("slab")
    me = region * slabs + slab
    cells = pl.ds(PAD, radial)

    load_b = pltpu.make_async_copy(mag_hbm, b_s.at[:, 1 : axial + 1, cells, :], load_sem.at[0])
    load_u = pltpu.make_async_copy(vel_hbm, u_s.at[:, 1 : axial + 1, cells, :], load_sem.at[1])
    load_w = pltpu.make_async_copy(wall_hbm, wall_s, load_sem.at[2])
    load_modes = pltpu.make_async_copy(mode_ref, mode_s, load_sem.at[3])
    load_layers = pltpu.make_async_copy(layer_ref, layer_s, load_sem.at[4])
    load_trace = pltpu.make_async_copy(
        mag_hbm.at[1:3, :, radial - 8 : radial, :], edge_s, load_sem.at[5]
    )
    load_modes.start()
    load_trace.start()
    load_b.start()
    load_u.start()
    load_layers.start()
    load_w.start()

    barrier = pltpu.get_barrier_semaphore()

    def each_other(act):
        for step in range(regions):
            its_region = lax.rem(region + step, regions)

            @pl.loop(0 if step else 1, slabs)
            def _(i, its_region=its_region):
                act(its_region, lax.rem(slab + i, slabs))

    def greet(its_region, its_slab):
        pl.semaphore_signal(
            barrier, inc=1, device_id=(its_region, its_slab), device_id_type=MESH
        )

    each_other(greet)

    shape = (radial, LANES)
    radius = 1.0 - (radial - iota(shape, 0).astype(F32) - 0.5) * RADIAL_STEP
    inverse = 1.0 / radius
    angle_step = 2.0 * math.pi / azimuth_total
    kr = TIME_STEP * DIFFUSIVITY / RADIAL_STEP**2
    kz = TIME_STEP * DIFFUSIVITY / AXIAL_STEP**2
    ar = TIME_STEP / (2.0 * RADIAL_STEP)
    az = TIME_STEP / (2.0 * AXIAL_STEP)
    kp = inverse * inverse * (TIME_STEP * DIFFUSIVITY / angle_step**2)
    radial_s[0] = inverse * (TIME_STEP / (2.0 * angle_step))
    radial_s[1] = kp
    radial_s[2] = inverse * (TIME_STEP * DIFFUSIVITY / (2.0 * RADIAL_STEP))
    radial_s[3] = (1.0 - 2.0 * kr - 2.0 * kz) - 2.0 * kp

    block_hi[...] = jnp.zeros(block_hi.shape, BF16)
    block_lo[...] = jnp.zeros(block_lo.shape, BF16)
    shape = (azimuth_total, per_row * LANES)
    picks = jnp.where(low(iota(shape, 0), per_row) == high(iota(shape, 1), LANES), 1.0, 0.0)
    shape = (slot_rows, azimuth_total)
    mine = high(iota(shape, 1), per_row) == iota(shape, 0)
    load_modes.wait()
    modes = mode_s[...].astype(F32)
    tens = jnp.floor(modes * (1.0 / 32.0))
    parts = [jnp.where(mine, part, 0.0) for part in (tens, modes - 32.0 * tens)]
    parts = jnp.dot(
        jnp.concatenate(parts, axis=0).astype(BF16),
        picks.astype(BF16),
        preferred_element_type=F32,
    )
    mode = 32.0 * parts[:slot_rows] + parts[slot_rows:]
    half = jnp.floor(mode * 0.5)
    odd = mode - 2.0 * half
    cell = region * LANES + low(iota(mode.shape, 1), LANES)
    turn = (half + odd) * (2 * cell + 1).astype(F32) - odd * (azimuth_total // 2)
    turn = turn * (0.5 / azimuth_total)
    turn = turn - jnp.floor(turn + 0.5)
    table = sine((0.25 - jnp.abs(turn)) * (2.0 * math.pi))
    table_hi, table_lo = split(table)

    load_trace.wait()
    for c in range(2):
        for z in range(axial):
            at = c * axial + z
            trace_s[at : at + 1, :] = edge_s[c, z, 7:8, :]
    trace_hi, trace_lo = split(trace_s[...])
    for q in range(per_row):
        block_hi[2 * axial * q : 2 * axial * (q + 1), LANES * q : LANES * (q + 1)] = trace_hi
        block_lo[2 * axial * q : 2 * axial * (q + 1), LANES * q : LANES * (q + 1)] = trace_lo
    both = jnp.concatenate([table_hi, table_lo], axis=0)
    turned = (((1,), (1,)), ((), ()))
    first = lax.dot_general(both, block_hi[...], turned, preferred_element_type=F32)
    second = lax.dot_general(table_hi, block_lo[...], turned, preferred_element_type=F32)
    coefficients = first[:slot_rows] + (first[slot_rows:] + second)
    for o in range(count):
        send1[o] = coefficients[rows_each * o : rows_each * (o + 1)]
    recv1[pl.ds(me, 1)] = send1[pl.ds(me, 1)]

    pl.semaphore_wait(barrier, count - 1)

    def send_coefficients(its_region, its_slab):
        pltpu.make_async_remote_copy(
            src_ref=send1.at[its_region * slabs + its_slab],
            dst_ref=recv1.at[me],
            send_sem=a2a_send.at[0],
            recv_sem=a2a_recv.at[0],
            device_id=(its_region, its_slab),
            device_id_type=MESH,
        ).start()

    each_other(send_coefficients)

    load_b.wait()
    load_u.wait()

    def axial_copy(field, at, up):
        return pltpu.make_async_remote_copy(
            src_ref=field.at[:, pl.ds(axial if up else 1, 1), cells, :],
            dst_ref=field.at[:, pl.ds(0 if up else axial + 1, 1), cells, :],
            send_sem=ax_send.at[at],
            recv_sem=ax_recv.at[at],
            device_id=(region, slab + 1 if up else slab - 1),
            device_id_type=MESH,
        )

    up_copies = [axial_copy(b_s, 0, True), axial_copy(u_s, 1, True)]
    down_copies = [axial_copy(b_s, 2, False), axial_copy(u_s, 3, False)]

    @pl.when(slab < slabs - 1)
    def _():
        for copy in up_copies:
            copy.start()

    @pl.when(slab > 0)
    def _():
        for copy in down_copies:
            copy.start()

    lane = iota((radial, LANES), 1)
    pair = high(low(lane + 1, LANES), 2)

    def pack(z, totals):
        totals = list(totals)
        for f, field in enumerate((b_s, u_s)):
            for c in range(3):
                at = c * axial + z
                plane = field[c, z + 1, PAD : PAD + radial, :]
                totals[f] = jnp.where(pair == at, pltpu.roll(plane, 2 * at, 1), totals[f])
                field[c, z + 1, PAD - 1 : PAD, :] = plane[0:1]
                field[c, z + 1, PAD + radial : PAD + radial + 1, :] = plane[radial - 1 : radial]
        return tuple(totals)

    nothing = jnp.zeros((radial, LANES), F32)
    pack_s[0], pack_s[1] = lax.fori_loop(0, axial, pack, (nothing, nothing), unroll=2)

    left = lax.rem(region + regions - 1, regions)
    right = lax.rem(region + 1, regions)

    def azimuth_copy(at, target):
        return pltpu.make_async_remote_copy(
            src_ref=pack_s,
            dst_ref=around_s.at[at],
            send_sem=az_send.at[at],
            recv_sem=az_recv.at[at],
            device_id=(target, slab),
            device_id_type=MESH,
        )

    azimuth_copies = [azimuth_copy(0, right)]
    if regions > 2:
        azimuth_copies.append(azimuth_copy(1, left))
    for copy in azimuth_copies:
        copy.start()

    single = (mode == 0.0) | (mode == azimuth_total - 1.0)
    weight_hi[...], weight_lo[...] = split(table * (jnp.where(single, 1.0, 2.0) / azimuth_total))

    @pl.when(slab == 0)
    def _():
        for field in (b_s, u_s):
            field[:, 0, PAD : PAD + radial, :] = jnp.zeros((3, radial, LANES), F32)

    @pl.when(slab == slabs - 1)
    def _():
        for field in (b_s, u_s):
            field[:, axial + 1, PAD : PAD + radial, :] = jnp.zeros((3, radial, LANES), F32)

    load_w.wait()

    @pl.loop(0, mode_count)
    def _(s):
        hi, lo = split(wall_s[s])
        at = pl.ds(pl.multiple_of(s * nz, nz), nz)
        whi_s[at, :] = hi
        wlo_s[at, :] = lo


    def wait_all(buffer, sem):
        part = buffer.at[pl.ds(0, count - 1)]
        pltpu.make_async_copy(part, part, sem).wait()

    for copy in azimuth_copies:
        copy.wait()

    even = low(lane, 2) == 0
    for f in range(2):
        from_left = around_s[0, f]
        from_right = around_s[len(azimuth_copies) - 1, f]
        halo_s[f] = jnp.where(
            even, pltpu.roll(from_left, 1, 1), pltpu.roll(from_right, LANES - 1, 1)
        )

    depth = 16
    first_row = PAD + slab // slabs
    first_lane = iota((depth, LANES), 1) == 0
    last_lane = iota((depth, LANES), 1) == LANES - 1

    def advance(turn, carry):
        z = lax.rem(turn, axial)
        for start in range(0, radial, depth):
            rows = slice(PAD + start, PAD + start + depth)
            above = pl.ds(first_row + (start + 1), depth)
            below = pl.ds(first_row + (start - 1), depth)
            here = slice(start, start + depth)
            ap = radial_s[0, here, :]
            kp = radial_s[1, here, :]
            k1 = radial_s[2, here, :]
            kc = radial_s[3, here, :]

            def around(f, c, center):
                shift = low(LANES - 2 * (c * axial + z), LANES)
                halo = pltpu.roll(halo_s[f, here, :], shift, 1)
                before = jnp.where(first_lane, halo, pltpu.roll(center, 1, 1))
                after = jnp.where(last_lane, halo, pltpu.roll(center, LANES - 1, 1))
                return before, after

            b = [b_s[c, z + 1, rows, :] for c in range(3)]
            u = [u_s[c, z + 1, rows, :] for c in range(3)]
            ur, up, uz = ar * u[0] - k1, ap * u[1], az * u[2]
            br, bp, bz = ar * b[0], ap * b[1], az * b[2]
            r_next, r_last = kr - ur, kr + ur
            p_next, p_last = kp - up, kp + up
            z_next, z_last = kz - uz, kz + uz
            for c in range(3):
                before, after = around(0, c, b[c])
                value = b[c] * kc
                value += r_next * b_s[c, z + 1, above, :] + r_last * b_s[c, z + 1, below, :]
                value += p_next * after + p_last * before
                value += z_next * b_s[c, z + 2, rows, :] + z_last * b_s[c, z, rows, :]
                before, after = around(1, c, u[c])
                value += br * (u_s[c, z + 1, above, :] - u_s[c, z + 1, below, :])
                value += bp * (after - before)
                value += bz * (u_s[c, z + 2, rows, :] - u_s[c, z, rows, :])
                out_s[c, z, here, :] = value
        return carry

    early = 3 * axial // 8
    lax.fori_loop(1, 1 + early, advance, 0, unroll=2)

    wait_all(recv1, a2a_recv.at[0])
    shape = (axial, LANES)
    own_cell = low(iota(shape, 1), axial) == iota(shape, 0)
    for j in range(slabs):
        got = recv1[j]
        for g in range(1, regions):
            got = got + recv1[g * slabs + j]
        for r in range(rows_each):
            hi, lo = split(jnp.where(own_cell, got[r : r + 1], 0.0))
            at = 2 * nz * r + axial * j
            spread_s[at : at + axial, :] = hi
            spread_s[at + nz : at + nz + axial, :] = lo
    shape = (LANES, LANES)
    group = jnp.where(high(iota(shape, 0), axial) == high(iota(shape, 1), axial), 1.0, 0.0).astype(BF16)
    shape = (nz, LANES)
    own_lane = low(iota(shape, 1), axial) == low(iota(shape, 0), axial)
    lane_group = high(iota(shape, 1), 2 * axial)
    repeated = jnp.dot(spread_s[...], group, preferred_element_type=F32).astype(BF16)
    for r in range(rows_each):
        hi = repeated[2 * nz * r : 2 * nz * r + nz]
        lo = repeated[2 * nz * r + nz : 2 * nz * (r + 1)]
        both = jnp.concatenate([hi, lo], axis=1)
        slots = slice(nz * per_row * r, nz * per_row * (r + 1))
        first = jnp.dot(whi_s[slots, :], both, preferred_element_type=F32)
        second = jnp.dot(wlo_s[slots, :], hi, preferred_element_type=F32)
        answer = first[:, :LANES] + (first[:, LANES:] + second)
        total = jnp.zeros((nz, LANES), F32)
        for q in range(per_row):
            part = answer[nz * q : nz * (q + 1)]
            total = jnp.where(own_lane & (lane_group == q), part, total)
        message = jnp.sum(total.reshape(slabs, axial, LANES), axis=1)
        for j in range(slabs):
            send2[j, r : r + 1, :] = message[j : j + 1]
    recv2[pl.ds(me, 1)] = send2[pl.ds(slab, 1)]

    def send_responses(its_region, its_slab):
        pltpu.make_async_remote_copy(
            src_ref=send2.at[its_slab],
            dst_ref=recv2.at[me],
            send_sem=a2a_send.at[1],
            recv_sem=a2a_recv.at[1],
            device_id=(its_region, its_slab),
            device_id_type=MESH,
        ).start()

    each_other(send_responses)

    @pl.when(slab < slabs - 1)
    def _():
        for copy in up_copies:
            copy.wait_send()
        for copy in down_copies:
            copy.wait_recv()

    @pl.when(slab > 0)
    def _():
        for copy in down_copies:
            copy.wait_send()
        for copy in up_copies:
            copy.wait_recv()

    lax.fori_loop(1 + early, axial + 1, advance, 0, unroll=2)
    load_layers.wait()
    for z in range(axial):
        trace_s[z : z + 1, :] = u_s[0, z + 1, PAD + radial - 1 : PAD + radial, :]
    outer = kr + radial_s[2, radial - 1 : radial, :] - ar * trace_s[0:axial, :]
    outer_s[...] = outer * (layer_s[...].astype(F32) * (1.0 / LW))
    wait_all(recv2, a2a_recv.at[1])
    for o in range(count):
        row_s[rows_each * o : rows_each * (o + 1), :] = recv2[o]
    wait_all(recv1, a2a_send.at[0])
    wait_all(recv2, a2a_send.at[1])


def finish_kernel(
    out_ref, row_ref, weight_hi, weight_lo, outer_ref, next_hbm, flux_hbm, edge_s, flux_s, sem
):
    _, axial, radial, _ = out_ref.shape
    top = radial - 8
    inner = pltpu.make_async_copy(
        out_ref.at[:, :, 0:top, :], next_hbm.at[:, :, 0:top, :], sem.at[0]
    )
    inner.start()
    hi, lo = split(row_ref[...].T)
    flux = jnp.zeros((2 * axial, LANES), F32)
    for q in range(LANES // (2 * axial)):
        part = slice(2 * axial * q, 2 * axial * (q + 1))
        lanes = slice(LANES * q, LANES * (q + 1))
        flux += jnp.dot(hi[part], weight_hi[:, lanes], preferred_element_type=F32)
        flux += jnp.dot(lo[part], weight_hi[:, lanes], preferred_element_type=F32)
        flux += jnp.dot(hi[part], weight_lo[:, lanes], preferred_element_type=F32)
    flux_s[...] = flux
    store_flux = pltpu.make_async_copy(flux_s, flux_hbm, sem.at[1])
    store_flux.start()
    outer = outer_ref[...]
    last = iota((8, LANES), 0) == 7
    for z in range(axial):
        edge_s[0, z] = out_ref[0, z, top:radial, :]
    for c in range(2):
        change = flux[axial * c : axial * (c + 1)] * outer
        for z in range(axial):
            edge = out_ref[c + 1, z, top:radial, :]
            edge_s[c + 1, z] = jnp.where(last, edge - change[z : z + 1], edge)
    store_edge = pltpu.make_async_copy(edge_s, next_hbm.at[:, :, top:radial, :], sem.at[2])
    store_edge.start()
    inner.wait()
    store_flux.wait()
    store_edge.wait()


def solution(mesh):
    regions = mesh.shape["region"]
    slabs = mesh.shape["slab"]
    count = regions * slabs

    def shards(magnetic, velocity, wall_response, mode_slots, wall_layers):
        _, axial, radial, azimuth = magnetic.shape
        azimuth_total = mode_slots.shape[0]
        mode_count, nz, _ = wall_response.shape
        rows_each = mode_count * 2 * axial // LANES
        per_row = LANES // (2 * axial)
        slot_rows = count * rows_each
        vmem = pl.BlockSpec(memory_space=pltpu.VMEM)
        hbm = pl.BlockSpec(memory_space=pltpu.HBM)
        field = pltpu.VMEM((3, axial + 2, radial + 2 * PAD, azimuth), F32)
        kept = pl.pallas_call(
            functools.partial(step_kernel, regions, slabs),
            out_shape=(
                pltpu.VMEM(magnetic.shape, F32),
                pltpu.VMEM((slot_rows, LANES), F32),
                pltpu.VMEM((slot_rows, per_row * LANES), BF16),
                pltpu.VMEM((slot_rows, per_row * LANES), BF16),
                pltpu.VMEM((axial, LANES), F32),
            ),
            in_specs=[hbm] * 5,
            out_specs=(vmem,) * 5,
            scratch_shapes=[
                field,
                field,
                pltpu.VMEM((1, azimuth_total), jnp.int32),
                pltpu.VMEM((1, azimuth), jnp.int32),
                pltpu.VMEM(wall_response.shape, F32),
                pltpu.VMEM((mode_count * nz, nz), BF16),
                pltpu.VMEM((mode_count * nz, nz), BF16),
                pltpu.VMEM((2, axial, 8, LANES), F32),
                pltpu.VMEM((2 * axial, LANES), F32),
                pltpu.VMEM((LANES, per_row * LANES), BF16),
                pltpu.VMEM((LANES, per_row * LANES), BF16),
                pltpu.VMEM((4, radial, LANES), F32),
                pltpu.VMEM((rows_each * 2 * nz, LANES), BF16),
                pltpu.VMEM((count, rows_each, LANES), F32),
                pltpu.VMEM((count, rows_each, LANES), F32),
                pltpu.VMEM((slabs, rows_each, LANES), F32),
                pltpu.VMEM((count, rows_each, LANES), F32),
                pltpu.VMEM((2, radial, LANES), F32),
                pltpu.VMEM((2, 2, radial, LANES), F32),
                pltpu.VMEM((2, radial, LANES), F32),
                pltpu.SemaphoreType.DMA((6,)),
                pltpu.SemaphoreType.DMA((2,)),
                pltpu.SemaphoreType.DMA((2,)),
                pltpu.SemaphoreType.DMA((4,)),
                pltpu.SemaphoreType.DMA((4,)),
                pltpu.SemaphoreType.DMA((2,)),
                pltpu.SemaphoreType.DMA((2,)),
            ],
            compiler_params=pltpu.CompilerParams(
                collective_id=0, has_side_effects=True, vmem_limit_bytes=48 * 1024 * 1024
            ),
            name="wall_step",
        )(
            *(
                pltpu.with_memory_space_constraint(x, pltpu.HBM)
                for x in (
                    mode_slots.reshape(1, azimuth_total),
                    wall_layers.reshape(1, azimuth),
                    magnetic,
                    velocity,
                    wall_response,
                )
            )
        )
        magnetic_next, flux = pl.pallas_call(
            finish_kernel,
            out_shape=(
                jax.ShapeDtypeStruct(magnetic.shape, F32),
                jax.ShapeDtypeStruct((2 * axial, azimuth), F32),
            ),
            in_specs=[vmem] * 5,
            out_specs=(hbm, hbm),
            scratch_shapes=[
                pltpu.VMEM((3, axial, 8, LANES), F32),
                pltpu.VMEM((2 * axial, LANES), F32),
                pltpu.SemaphoreType.DMA((3,)),
            ],
            compiler_params=pltpu.CompilerParams(vmem_limit_bytes=48 * 1024 * 1024),
            name="wall_finish",
        )(*(pltpu.with_memory_space_constraint(x, pltpu.VMEM) for x in kept))
        return magnetic_next, flux.reshape(2, axial, azimuth)

    placed = (
        P(None, "slab", None, "region"),
        P(None, "slab", None, "region"),
        P(("region", "slab"), None, None),
        P(),
        P("region"),
    )
    return jax.shard_map(
        shards,
        mesh=mesh,
        in_specs=placed,
        out_specs=(P(None, "slab", None, "region"), P(None, "slab", "region")),
        check_vma=False,
    )
```

```python
import functools
import math

import jax
import jax.numpy as jnp
from jax import lax
from jax.experimental import pallas as pl
from jax.experimental.pallas import tpu as pltpu
from jax.sharding import PartitionSpec as P

LW = 8
TIME_STEP = 0.0003
DIFFUSIVITY = 0.001
RADIAL_STEP = 1.0 / 384.0
AXIAL_STEP = 1.0 / 768.0
MESH = pl.DeviceIdType.MESH
F32 = jnp.float32
BF16 = jnp.bfloat16

PAD = 8
LANES = 128


def iota(shape, dim):
    return lax.broadcasted_iota(jnp.int32, shape, dim)


def high(x, n):
    if n & (n - 1):
        return x // n
    return lax.shift_right_logical(x, jnp.full(x.shape, n.bit_length() - 1, x.dtype))


def low(x, n):
    return lax.rem(x, n) if n & (n - 1) else x & (n - 1)


def split(x):
    hi = x.astype(BF16)
    return hi, (x - hi.astype(F32)).astype(BF16)


def sine(t):
    s = t * t
    value = 1.0 / math.factorial(13)
    for n in (11, 9, 7, 5, 3, 1):
        sign = 1.0 if (n // 2) % 2 == 0 else -1.0
        value = value * s + sign / math.factorial(n)
    return value * t


def step_kernel(
    regions,
    slabs,
    mode_ref,
    layer_ref,
    mag_hbm,
    vel_hbm,
    wall_hbm,
    out_s,
    row_s,
    weight_hi,
    weight_lo,
    outer_s,
    b_s,
    u_s,
    mode_s,
    layer_s,
    wall_s,
    whi_s,
    wlo_s,
    edge_s,
    trace_s,
    block_hi,
    block_lo,
    radial_s,
    spread_s,
    send1,
    recv1,
    send2,
    recv2,
    pack_s,
    around_s,
    halo_s,
    load_sem,
    a2a_send,
    a2a_recv,
    ax_send,
    ax_recv,
    az_send,
    az_recv,
):
    count = regions * slabs
    radial = mag_hbm.shape[2]
    axial = mag_hbm.shape[1]
    azimuth_total = mode_s.shape[1]
    mode_count, nz, _ = wall_hbm.shape
    rows_each = send1.shape[1]
    slot_rows = count * rows_each
    per_row = LANES // (2 * axial)
    region = lax.axis_index("region")
    slab = lax.axis_index("slab")
    me = region * slabs + slab
    cells = pl.ds(PAD, radial)

    load_b = pltpu.make_async_copy(mag_hbm, b_s.at[:, 1 : axial + 1, cells, :], load_sem.at[0])
    load_u = pltpu.make_async_copy(vel_hbm, u_s.at[:, 1 : axial + 1, cells, :], load_sem.at[1])
    load_w = pltpu.make_async_copy(wall_hbm, wall_s, load_sem.at[2])
    load_modes = pltpu.make_async_copy(mode_ref, mode_s, load_sem.at[3])
    load_layers = pltpu.make_async_copy(layer_ref, layer_s, load_sem.at[4])
    load_trace = pltpu.make_async_copy(
        mag_hbm.at[1:3, :, radial - 8 : radial, :], edge_s, load_sem.at[5]
    )
    load_modes.start()
    load_trace.start()
    load_b.start()
    load_u.start()
    load_layers.start()
    load_w.start()

    barrier = pltpu.get_barrier_semaphore()

    def each_other(act):
        for step in range(regions):
            its_region = lax.rem(region + step, regions)

            @pl.loop(0 if step else 1, slabs)
            def _(i, its_region=its_region):
                act(its_region, lax.rem(slab + i, slabs))

    def greet(its_region, its_slab):
        pl.semaphore_signal(
            barrier, inc=1, device_id=(its_region, its_slab), device_id_type=MESH
        )

    each_other(greet)

    shape = (radial, LANES)
    radius = 1.0 - (radial - iota(shape, 0).astype(F32) - 0.5) * RADIAL_STEP
    inverse = 1.0 / radius
    angle_step = 2.0 * math.pi / azimuth_total
    kr = TIME_STEP * DIFFUSIVITY / RADIAL_STEP**2
    kz = TIME_STEP * DIFFUSIVITY / AXIAL_STEP**2
    ar = TIME_STEP / (2.0 * RADIAL_STEP)
    az = TIME_STEP / (2.0 * AXIAL_STEP)
    kp = inverse * inverse * (TIME_STEP * DIFFUSIVITY / angle_step**2)
    radial_s[0] = inverse * (TIME_STEP / (2.0 * angle_step))
    radial_s[1] = kp
    radial_s[2] = inverse * (TIME_STEP * DIFFUSIVITY / (2.0 * RADIAL_STEP))
    radial_s[3] = (1.0 - 2.0 * kr - 2.0 * kz) - 2.0 * kp

    block_hi[...] = jnp.zeros(block_hi.shape, BF16)
    block_lo[...] = jnp.zeros(block_lo.shape, BF16)
    shape = (azimuth_total, per_row * LANES)
    picks = jnp.where(low(iota(shape, 0), per_row) == high(iota(shape, 1), LANES), 1.0, 0.0)
    shape = (slot_rows, azimuth_total)
    mine = high(iota(shape, 1), per_row) == iota(shape, 0)
    load_modes.wait()
    modes = mode_s[...].astype(F32)
    tens = jnp.floor(modes * (1.0 / 32.0))
    parts = [jnp.where(mine, part, 0.0) for part in (tens, modes - 32.0 * tens)]
    parts = jnp.dot(
        jnp.concatenate(parts, axis=0).astype(BF16),
        picks.astype(BF16),
        preferred_element_type=F32,
    )
    mode = 32.0 * parts[:slot_rows] + parts[slot_rows:]
    half = jnp.floor(mode * 0.5)
    odd = mode - 2.0 * half
    cell = region * LANES + low(iota(mode.shape, 1), LANES)
    turn = (half + odd) * (2 * cell + 1).astype(F32) - odd * (azimuth_total // 2)
    turn = turn * (0.5 / azimuth_total)
    turn = turn - jnp.floor(turn + 0.5)
    table = sine((0.25 - jnp.abs(turn)) * (2.0 * math.pi))
    table_hi, table_lo = split(table)

    load_trace.wait()
    for c in range(2):
        for z in range(axial):
            at = c * axial + z
            trace_s[at : at + 1, :] = edge_s[c, z, 7:8, :]
    trace_hi, trace_lo = split(trace_s[...])
    for q in range(per_row):
        block_hi[2 * axial * q : 2 * axial * (q + 1), LANES * q : LANES * (q + 1)] = trace_hi
        block_lo[2 * axial * q : 2 * axial * (q + 1), LANES * q : LANES * (q + 1)] = trace_lo
    both = jnp.concatenate([table_hi, table_lo], axis=0)
    turned = (((1,), (1,)), ((), ()))
    first = lax.dot_general(both, block_hi[...], turned, preferred_element_type=F32)
    second = lax.dot_general(table_hi, block_lo[...], turned, preferred_element_type=F32)
    coefficients = first[:slot_rows] + (first[slot_rows:] + second)
    for o in range(count):
        send1[o] = coefficients[rows_each * o : rows_each * (o + 1)]
    recv1[pl.ds(me, 1)] = send1[pl.ds(me, 1)]

    pl.semaphore_wait(barrier, count - 1)

    def send_coefficients(its_region, its_slab):
        pltpu.make_async_remote_copy(
            src_ref=send1.at[its_region * slabs + its_slab],
            dst_ref=recv1.at[me],
            send_sem=a2a_send.at[0],
            recv_sem=a2a_recv.at[0],
            device_id=(its_region, its_slab),
            device_id_type=MESH,
        ).start()

    each_other(send_coefficients)

    load_b.wait()
    load_u.wait()

    def axial_copy(field, at, up):
        return pltpu.make_async_remote_copy(
            src_ref=field.at[:, pl.ds(axial if up else 1, 1), cells, :],
            dst_ref=field.at[:, pl.ds(0 if up else axial + 1, 1), cells, :],
            send_sem=ax_send.at[at],
            recv_sem=ax_recv.at[at],
            device_id=(region, slab + 1 if up else slab - 1),
            device_id_type=MESH,
        )

    up_copies = [axial_copy(b_s, 0, True), axial_copy(u_s, 1, True)]
    down_copies = [axial_copy(b_s, 2, False), axial_copy(u_s, 3, False)]

    lane = iota((radial, LANES), 1)
    pair = high(low(lane + 1, LANES), 2)

    def pack(z, totals):
        totals = list(totals)
        for f, field in enumerate((b_s, u_s)):
            for c in range(3):
                at = c * axial + z
                plane = field[c, z + 1, PAD : PAD + radial, :]
                totals[f] = jnp.where(pair == at, pltpu.roll(plane, 2 * at, 1), totals[f])
                field[c, z + 1, PAD - 1 : PAD, :] = plane[0:1]
                field[c, z + 1, PAD + radial : PAD + radial + 1, :] = plane[radial - 1 : radial]
        return tuple(totals)

    nothing = jnp.zeros((radial, LANES), F32)
    pack_s[0], pack_s[1] = lax.fori_loop(0, axial, pack, (nothing, nothing), unroll=2)

    left = lax.rem(region + regions - 1, regions)
    right = lax.rem(region + 1, regions)

    def azimuth_copy(at, target):
        return pltpu.make_async_remote_copy(
            src_ref=pack_s,
            dst_ref=around_s.at[at],
            send_sem=az_send.at[at],
            recv_sem=az_recv.at[at],
            device_id=(target, slab),
            device_id_type=MESH,
        )

    azimuth_copies = [azimuth_copy(0, right)]
    if regions > 2:
        azimuth_copies.append(azimuth_copy(1, left))
    for copy in azimuth_copies:
        copy.start()

    @pl.when(slab < slabs - 1)
    def _():
        for copy in up_copies:
            copy.start()

    @pl.when(slab > 0)
    def _():
        for copy in down_copies:
            copy.start()

    single = (mode == 0.0) | (mode == azimuth_total - 1.0)
    weight_hi[...], weight_lo[...] = split(table * (jnp.where(single, 1.0, 2.0) / azimuth_total))

    @pl.when(slab == 0)
    def _():
        for field in (b_s, u_s):
            field[:, 0, PAD : PAD + radial, :] = jnp.zeros((3, radial, LANES), F32)

    @pl.when(slab == slabs - 1)
    def _():
        for field in (b_s, u_s):
            field[:, axial + 1, PAD : PAD + radial, :] = jnp.zeros((3, radial, LANES), F32)

    load_w.wait()

    @pl.loop(0, mode_count)
    def _(s):
        hi, lo = split(wall_s[s])
        at = pl.ds(pl.multiple_of(s * nz, nz), nz)
        whi_s[at, :] = hi
        wlo_s[at, :] = lo


    def wait_all(buffer, sem):
        part = buffer.at[pl.ds(0, count - 1)]
        pltpu.make_async_copy(part, part, sem).wait()

    for copy in azimuth_copies:
        copy.wait()

    even = low(lane, 2) == 0
    for f in range(2):
        from_left = around_s[0, f]
        from_right = around_s[len(azimuth_copies) - 1, f]
        halo_s[f] = jnp.where(
            even, pltpu.roll(from_left, 1, 1), pltpu.roll(from_right, LANES - 1, 1)
        )

    depth = 16
    first_row = PAD + slab // slabs
    first_lane = iota((depth, LANES), 1) == 0
    last_lane = iota((depth, LANES), 1) == LANES - 1

    def advance(turn, carry):
        z = lax.rem(turn, axial)
        for start in range(0, radial, depth):
            rows = slice(PAD + start, PAD + start + depth)
            above = pl.ds(first_row + (start + 1), depth)
            below = pl.ds(first_row + (start - 1), depth)
            here = slice(start, start + depth)
            ap = radial_s[0, here, :]
            kp = radial_s[1, here, :]
            k1 = radial_s[2, here, :]
            kc = radial_s[3, here, :]

            def around(f, c, center):
                shift = low(LANES - 2 * (c * axial + z), LANES)
                halo = pltpu.roll(halo_s[f, here, :], shift, 1)
                before = jnp.where(first_lane, halo, pltpu.roll(center, 1, 1))
                after = jnp.where(last_lane, halo, pltpu.roll(center, LANES - 1, 1))
                return before, after

            b = [b_s[c, z + 1, rows, :] for c in range(3)]
            u = [u_s[c, z + 1, rows, :] for c in range(3)]
            ur, up, uz = ar * u[0] - k1, ap * u[1], az * u[2]
            br, bp, bz = ar * b[0], ap * b[1], az * b[2]
            r_next, r_last = kr - ur, kr + ur
            p_next, p_last = kp - up, kp + up
            z_next, z_last = kz - uz, kz + uz
            for c in range(3):
                before, after = around(0, c, b[c])
                value = b[c] * kc
                value += r_next * b_s[c, z + 1, above, :] + r_last * b_s[c, z + 1, below, :]
                value += p_next * after + p_last * before
                value += z_next * b_s[c, z + 2, rows, :] + z_last * b_s[c, z, rows, :]
                before, after = around(1, c, u[c])
                value += br * (u_s[c, z + 1, above, :] - u_s[c, z + 1, below, :])
                value += bp * (after - before)
                value += bz * (u_s[c, z + 2, rows, :] - u_s[c, z, rows, :])
                out_s[c, z, here, :] = value
        return carry

    early = axial // 8
    lax.fori_loop(1, 1 + early, advance, 0, unroll=2)

    wait_all(recv1, a2a_recv.at[0])
    shape = (axial, LANES)
    own_cell = low(iota(shape, 1), axial) == iota(shape, 0)
    for j in range(slabs):
        got = recv1[j]
        for g in range(1, regions):
            got = got + recv1[g * slabs + j]
        for r in range(rows_each):
            hi, lo = split(jnp.where(own_cell, got[r : r + 1], 0.0))
            at = 2 * nz * r + axial * j
            spread_s[at : at + axial, :] = hi
            spread_s[at + nz : at + nz + axial, :] = lo
    shape = (LANES, LANES)
    group = jnp.where(high(iota(shape, 0), axial) == high(iota(shape, 1), axial), 1.0, 0.0).astype(BF16)
    shape = (nz, LANES)
    own_lane = low(iota(shape, 1), axial) == low(iota(shape, 0), axial)
    lane_group = high(iota(shape, 1), 2 * axial)
    repeated = jnp.dot(spread_s[...], group, preferred_element_type=F32).astype(BF16)
    for r in range(rows_each):
        hi = repeated[2 * nz * r : 2 * nz * r + nz]
        lo = repeated[2 * nz * r + nz : 2 * nz * (r + 1)]
        both = jnp.concatenate([hi, lo], axis=1)
        slots = slice(nz * per_row * r, nz * per_row * (r + 1))
        first = jnp.dot(whi_s[slots, :], both, preferred_element_type=F32)
        second = jnp.dot(wlo_s[slots, :], hi, preferred_element_type=F32)
        answer = first[:, :LANES] + (first[:, LANES:] + second)
        total = jnp.zeros((nz, LANES), F32)
        for q in range(per_row):
            part = answer[nz * q : nz * (q + 1)]
            total = jnp.where(own_lane & (lane_group == q), part, total)
        message = jnp.sum(total.reshape(slabs, axial, LANES), axis=1)
        for j in range(slabs):
            send2[j, r : r + 1, :] = message[j : j + 1]
    recv2[pl.ds(me, 1)] = send2[pl.ds(slab, 1)]

    def send_responses(its_region, its_slab):
        pltpu.make_async_remote_copy(
            src_ref=send2.at[its_slab],
            dst_ref=recv2.at[me],
            send_sem=a2a_send.at[1],
            recv_sem=a2a_recv.at[1],
            device_id=(its_region, its_slab),
            device_id_type=MESH,
        ).start()

    each_other(send_responses)

    lax.fori_loop(1 + early, axial - 1, advance, 0, unroll=2)

    @pl.when(slab < slabs - 1)
    def _():
        for copy in up_copies:
            copy.wait_send()
        for copy in down_copies:
            copy.wait_recv()

    @pl.when(slab > 0)
    def _():
        for copy in down_copies:
            copy.wait_send()
        for copy in up_copies:
            copy.wait_recv()

    lax.fori_loop(axial - 1, axial + 1, advance, 0, unroll=2)
    load_layers.wait()
    for z in range(axial):
        trace_s[z : z + 1, :] = u_s[0, z + 1, PAD + radial - 1 : PAD + radial, :]
    outer = kr + radial_s[2, radial - 1 : radial, :] - ar * trace_s[0:axial, :]
    outer_s[...] = outer * (layer_s[...].astype(F32) * (1.0 / LW))
    wait_all(recv2, a2a_recv.at[1])
    for o in range(count):
        row_s[rows_each * o : rows_each * (o + 1), :] = recv2[o]
    wait_all(recv1, a2a_send.at[0])
    wait_all(recv2, a2a_send.at[1])


def finish_kernel(
    out_ref, row_ref, weight_hi, weight_lo, outer_ref, next_hbm, flux_hbm, edge_s, flux_s, sem
):
    _, axial, radial, _ = out_ref.shape
    top = radial - 8
    inner = pltpu.make_async_copy(
        out_ref.at[:, :, 0:top, :], next_hbm.at[:, :, 0:top, :], sem.at[0]
    )
    inner.start()
    hi, lo = split(row_ref[...].T)
    flux = jnp.zeros((2 * axial, LANES), F32)
    for q in range(LANES // (2 * axial)):
        part = slice(2 * axial * q, 2 * axial * (q + 1))
        lanes = slice(LANES * q, LANES * (q + 1))
        flux += jnp.dot(hi[part], weight_hi[:, lanes], preferred_element_type=F32)
        flux += jnp.dot(lo[part], weight_hi[:, lanes], preferred_element_type=F32)
        flux += jnp.dot(hi[part], weight_lo[:, lanes], preferred_element_type=F32)
    flux_s[...] = flux
    store_flux = pltpu.make_async_copy(flux_s, flux_hbm, sem.at[1])
    store_flux.start()
    outer = outer_ref[...]
    last = iota((8, LANES), 0) == 7
    for z in range(axial):
        edge_s[0, z] = out_ref[0, z, top:radial, :]
    for c in range(2):
        change = flux[axial * c : axial * (c + 1)] * outer
        for z in range(axial):
            edge = out_ref[c + 1, z, top:radial, :]
            edge_s[c + 1, z] = jnp.where(last, edge - change[z : z + 1], edge)
    store_edge = pltpu.make_async_copy(edge_s, next_hbm.at[:, :, top:radial, :], sem.at[2])
    store_edge.start()
    inner.wait()
    store_flux.wait()
    store_edge.wait()


def solution(mesh):
    regions = mesh.shape["region"]
    slabs = mesh.shape["slab"]
    count = regions * slabs

    def shards(magnetic, velocity, wall_response, mode_slots, wall_layers):
        _, axial, radial, azimuth = magnetic.shape
        azimuth_total = mode_slots.shape[0]
        mode_count, nz, _ = wall_response.shape
        rows_each = mode_count * 2 * axial // LANES
        per_row = LANES // (2 * axial)
        slot_rows = count * rows_each
        vmem = pl.BlockSpec(memory_space=pltpu.VMEM)
        hbm = pl.BlockSpec(memory_space=pltpu.HBM)
        field = pltpu.VMEM((3, axial + 2, radial + 2 * PAD, azimuth), F32)
        kept = pl.pallas_call(
            functools.partial(step_kernel, regions, slabs),
            out_shape=(
                pltpu.VMEM(magnetic.shape, F32),
                pltpu.VMEM((slot_rows, LANES), F32),
                pltpu.VMEM((slot_rows, per_row * LANES), BF16),
                pltpu.VMEM((slot_rows, per_row * LANES), BF16),
                pltpu.VMEM((axial, LANES), F32),
            ),
            in_specs=[hbm] * 5,
            out_specs=(vmem,) * 5,
            scratch_shapes=[
                field,
                field,
                pltpu.VMEM((1, azimuth_total), jnp.int32),
                pltpu.VMEM((1, azimuth), jnp.int32),
                pltpu.VMEM(wall_response.shape, F32),
                pltpu.VMEM((mode_count * nz, nz), BF16),
                pltpu.VMEM((mode_count * nz, nz), BF16),
                pltpu.VMEM((2, axial, 8, LANES), F32),
                pltpu.VMEM((2 * axial, LANES), F32),
                pltpu.VMEM((LANES, per_row * LANES), BF16),
                pltpu.VMEM((LANES, per_row * LANES), BF16),
                pltpu.VMEM((4, radial, LANES), F32),
                pltpu.VMEM((rows_each * 2 * nz, LANES), BF16),
                pltpu.VMEM((count, rows_each, LANES), F32),
                pltpu.VMEM((count, rows_each, LANES), F32),
                pltpu.VMEM((slabs, rows_each, LANES), F32),
                pltpu.VMEM((count, rows_each, LANES), F32),
                pltpu.VMEM((2, radial, LANES), F32),
                pltpu.VMEM((2, 2, radial, LANES), F32),
                pltpu.VMEM((2, radial, LANES), F32),
                pltpu.SemaphoreType.DMA((6,)),
                pltpu.SemaphoreType.DMA((2,)),
                pltpu.SemaphoreType.DMA((2,)),
                pltpu.SemaphoreType.DMA((4,)),
                pltpu.SemaphoreType.DMA((4,)),
                pltpu.SemaphoreType.DMA((2,)),
                pltpu.SemaphoreType.DMA((2,)),
            ],
            compiler_params=pltpu.CompilerParams(
                collective_id=0, has_side_effects=True, vmem_limit_bytes=48 * 1024 * 1024
            ),
            name="wall_step",
        )(
            *(
                pltpu.with_memory_space_constraint(x, pltpu.HBM)
                for x in (
                    mode_slots.reshape(1, azimuth_total),
                    wall_layers.reshape(1, azimuth),
                    magnetic,
                    velocity,
                    wall_response,
                )
            )
        )
        magnetic_next, flux = pl.pallas_call(
            finish_kernel,
            out_shape=(
                jax.ShapeDtypeStruct(magnetic.shape, F32),
                jax.ShapeDtypeStruct((2 * axial, azimuth), F32),
            ),
            in_specs=[vmem] * 5,
            out_specs=(hbm, hbm),
            scratch_shapes=[
                pltpu.VMEM((3, axial, 8, LANES), F32),
                pltpu.VMEM((2 * axial, LANES), F32),
                pltpu.SemaphoreType.DMA((3,)),
            ],
            compiler_params=pltpu.CompilerParams(vmem_limit_bytes=48 * 1024 * 1024),
            name="wall_finish",
        )(*(pltpu.with_memory_space_constraint(x, pltpu.VMEM) for x in kept))
        return magnetic_next, flux.reshape(2, axial, azimuth)

    placed = (
        P(None, "slab", None, "region"),
        P(None, "slab", None, "region"),
        P(("region", "slab"), None, None),
        P(),
        P("region"),
    )
    return jax.shard_map(
        shards,
        mesh=mesh,
        in_specs=placed,
        out_specs=(P(None, "slab", None, "region"), P(None, "slab", "region")),
        check_vma=False,
    )
```
